256 devices in a mesh: gx: 8 (over y, core), gz: 32 (over z, x).
Axes of the slice: x: 4, y: 4, z: 8, core: 2. Of those that a mesh axis runs over, the one named last changes fastest.
Arguments:
- velocity: float32 [4, 12288, 8192], P(None, 'gx', 'gz'), may hold values from -6 to 6
Outputs:
- derivative_sum: float32 [4, 12288, 8192], P(None, 'gx', 'gz')
The draws below stay inside these ranges and needn't reach their ends.
All inputs are finite; a program needn't handle non-finite values.
Results may differ from the reference program's by a relative error of at most 0.000054.
Values sent between devices are 32-bit elements; how exact they have to be, the bound alone decides.
No kernel may reach another device: no remote copies, remote signals or barrier semaphores. Data moves between devices by JAX's collectives and lax.ppermute only.
A program may use at most 64 MiB of HBM per device.

```python
import jax
import jax.numpy as jnp
from jax import lax

FIELDS = 4
NX = 12288
NZ = 8192


def steps_of(key, dims, split, smallest, top_value):
    gain, own = 1.0, jax.random.fold_in(key, 6)
    for dim, blocks in split:
        heights = jnp.exp(jax.random.uniform(jax.random.fold_in(own, dim), (blocks,), jnp.float32, smallest / len(split), top_value / len(split)))
        gain = gain * jnp.repeat(heights, dims[dim] // blocks).reshape([-1 if axis == dim else 1 for axis in range(len(dims))])
    return gain


def centred(stream_key, shape, scale, limit, split=(), dtype=jnp.bfloat16):
    factor_of = steps_of(stream_key, shape, split, -0.22, 0.18) if split else 1.0
    entries = jax.random.normal(stream_key, shape, jnp.float32) * scale * factor_of
    return jnp.minimum(jnp.maximum(entries, -limit), limit).astype(dtype)


def setup_inputs(seed: int = 0) -> dict:
    key_of = jax.random.split(jax.random.key(seed), 2)
    velocity = centred(key_of[0], (FIELDS, NX, NZ), 1.0, 6.0, ((1, 8), (2, 32)), jnp.float32)
    return {"velocity": velocity}


def streamwise(field):
    spectrum = jnp.fft.rfft(field, axis=0)
    wavenum = 2.0 * jnp.pi * jnp.arange(NX // 2 + 1).astype(jnp.float32) / NX
    factor = ((14.0 / 9.0) * jnp.sin(wavenum) + (1.0 / 18.0) * jnp.sin(2.0 * wavenum)) / (1.0 + (2.0 / 3.0) * jnp.cos(wavenum))
    return jnp.fft.irfft(spectrum * (1j * factor)[:, None], n=NX, axis=0).astype(jnp.float32)


def spanwise(field):
    first = jnp.roll(field, -1, axis=1) - jnp.roll(field, 1, axis=1)
    second = jnp.roll(field, -2, axis=1) - jnp.roll(field, 2, axis=1)
    third = jnp.roll(field, -3, axis=1) - jnp.roll(field, 3, axis=1)
    return 0.75 * first - 0.15 * second + (1.0 / 60.0) * third


def reference(velocity):
    def single(field):
        return streamwise(field) + spanwise(field)
    return lax.map(single, velocity)
```

```python
import math

import jax
import jax.numpy as jnp
import numpy as np
from jax import lax
from jax.experimental import pallas as pl
from jax.experimental.pallas import tpu as pltpu
from jax.sharding import PartitionSpec as P

FIELDS, ROWS, LANES = 4, 1536, 256
HALO = 24
PAD = HALO + ROWS + HALO
SUB = 8
CHUNK = ROWS // SUB
WARM = HALO - 2
TILE = 128
BLOCKS = ROWS // TILE
RATIO = (math.sqrt(5.0) - 3.0) / 2.0
KAPPA = -1.0 / (3.0 * RATIO)
NEAR = 7.0 / 9.0 / KAPPA
FAR = 1.0 / 36.0 / KAPPA
MIB = 1 << 20


def edge_matrices():
    def green(m):
        return RATIO ** np.abs(m) / (KAPPA * (1.0 - RATIO * RATIO))

    def weight(m):
        return 7.0 / 9.0 * (green(m + 1) - green(m - 1)) + 1.0 / 36.0 * (green(m + 2) - green(m - 2))

    here = np.arange(HALO)[:, None]
    there = np.arange(HALO)[None, :]
    top = weight(here - (there - HALO))
    bottom = weight(here - (there + HALO))
    return top.astype(np.float32), bottom.astype(np.float32)


def pack_kernel(v_hbm, pad, head, tail, first, last, sems):
    copies = []
    for f in range(FIELDS):
        for c in range(2):
            lanes = pl.ds(c * TILE, TILE)
            copy = pltpu.make_async_copy(v_hbm.at[f, :, lanes], pad.at[f, c, pl.ds(HALO, ROWS)], sems.at[f, c])
            copy.start()
            copies.append(copy)
    zeros = jnp.zeros((HALO, TILE), jnp.float32)
    for f in range(FIELDS):
        for c in range(2):
            pad[f, c, pl.ds(0, HALO)] = zeros
            pad[f, c, pl.ds(HALO + ROWS, HALO)] = zeros
    lane = lax.broadcasted_iota(jnp.int32, (TILE, TILE), 1)
    for f in range(FIELDS):
        for c in range(2):
            copies[2 * f + c].wait()
            head[pl.ds(f * HALO, HALO), c * TILE : (c + 1) * TILE] = pad[f, c, pl.ds(HALO, HALO)]
            tail[pl.ds(f * HALO, HALO), c * TILE : (c + 1) * TILE] = pad[f, c, pl.ds(ROWS, HALO)]
        for b in range(BLOCKS):
            rows = pl.ds(HALO + b * TILE, TILE)
            both = jnp.where(lane < 64, pad[f, 0, rows], pad[f, 1, rows])
            turned = both.T
            at = pl.ds((f * BLOCKS + b) * 4, 4)
            first[at] = turned[0:4]
            last[at] = turned[TILE - 4 :]


def difference_matrix():
    gap = lax.broadcasted_iota(jnp.int32, (LANES, LANES), 0) - lax.broadcasted_iota(
        jnp.int32, (LANES, LANES), 1
    )
    size = jnp.abs(gap)
    weight = jnp.where(size == 1, 45.0, jnp.where(size == 2, -9.0, jnp.where(size == 3, 1.0, 0.0)))
    return jnp.where(gap < 0, -weight, weight).astype(jnp.bfloat16)


def inner_kernel(pad, out, swept):
    unroll = 4
    for f in range(0, FIELDS, 2):
        chains = [(g, c) for g in (f, f + 1) for c in (0, 1)]

        def row(chain, k):
            g, c = chain
            return pad[g, c, pl.ds(k, SUB, stride=CHUNK)]

        def forward(step, carry):
            carry = list(carry)
            for u in range(unroll):
                k = step * unroll + u
                for n, chain in enumerate(chains):
                    back2, back1, here, ahead1, y = carry[n]
                    ahead2 = row(chain, k + 4)
                    y = RATIO * y + (NEAR * (ahead1 - back1) + FAR * (ahead2 - back2))
                    swept[n, pl.ds(pl.multiple_of(k * SUB, SUB), SUB)] = y
                    carry[n] = (back1, here, ahead1, ahead2, y)
            return tuple(carry)

        start = tuple(
            tuple(row(chain, j) for j in range(4)) + (jnp.zeros((SUB, TILE), jnp.float32),)
            for chain in chains
        )
        steps = WARM + CHUNK + WARM
        lax.fori_loop(0, steps // unroll, forward, start)

        def value(n, k):
            return swept[n, pl.ds(pl.multiple_of(k * SUB, SUB), SUB)]

        def warm(step, carry):
            k = steps - 1 - step
            return tuple(RATIO * carry[n] + value(n, k) for n in range(4))

        def backward(step, carry):
            carry = list(carry)
            for u in range(unroll):
                k = CHUNK - 1 - (step * unroll + u)
                for n, (g, c) in enumerate(chains):
                    carry[n] = RATIO * carry[n] + value(n, k + WARM)
                    out[g, c, pl.ds(k, SUB, stride=CHUNK)] = carry[n]
            return tuple(carry)

        zero = tuple(jnp.zeros((SUB, TILE), jnp.float32) for _ in chains)
        carry = lax.fori_loop(0, WARM, warm, zero, unroll=True)
        lax.fori_loop(0, CHUNK // unroll, backward, carry)

    matrix = difference_matrix()
    for f in range(FIELDS):
        for b in range(0, ROWS, 256):
            rows = pl.ds(HALO + b, 256)
            here = jnp.concatenate([pad[f, 0, rows], pad[f, 1, rows]], axis=1)
            high = here.astype(jnp.bfloat16)
            rest = here - high.astype(jnp.float32)
            middle = rest.astype(jnp.bfloat16)
            low = (rest - middle.astype(jnp.float32)).astype(jnp.bfloat16)
            total = jnp.dot(high, matrix, preferred_element_type=jnp.float32)
            total += jnp.dot(middle, matrix, preferred_element_type=jnp.float32)
            total += jnp.dot(low, matrix, preferred_element_type=jnp.float32)
            total = total * (1.0 / 60.0)
            out[f, 0, pl.ds(b, 256)] += total[:, 0:TILE]
            out[f, 1, pl.ds(b, 256)] += total[:, TILE:]


def edge_kernel(inner, before, after, left, right, top, bottom, out_hbm, work, sems):
    copies = []
    zeros = jnp.zeros((TILE - 8, TILE), jnp.float32)
    none = jnp.zeros((1, TILE), jnp.float32)
    lane = lax.broadcasted_iota(jnp.int32, (TILE, TILE), 1)
    for f in range(FIELDS):
        for b in range(BLOCKS):
            at = (f * BLOCKS + b) * 4
            l3, l2, l1 = (left[pl.ds(at + n, 1)] for n in (1, 2, 3))
            r1, r2, r3 = (right[pl.ds(at + n, 1)] for n in (0, 1, 2))
            low = jnp.concatenate(
                [
                    -0.75 * l1 + 0.15 * l2 - l3 * (1.0 / 60.0),
                    0.15 * l1 - l2 * (1.0 / 60.0),
                    l1 * (-1.0 / 60.0),
                    none,
                ]
            )
            high = jnp.concatenate(
                [
                    none,
                    r1 * (1.0 / 60.0),
                    -0.15 * r1 + r2 * (1.0 / 60.0),
                    0.75 * r1 - 0.15 * r2 + r3 * (1.0 / 60.0),
                ]
            )
            turned = jnp.concatenate([low, zeros, high]).T
            rows = pl.ds(b * TILE, TILE)
            work[f, 0, rows] = inner[f, 0, rows] + jnp.where(lane < 64, turned, 0.0)
            work[f, 1, rows] = inner[f, 1, rows] + jnp.where(lane < 64, 0.0, turned)
        halo = pl.ds(f * HALO, HALO)
        low = jnp.dot(
            top[...], before[halo], precision=lax.Precision.HIGHEST, preferred_element_type=jnp.float32
        )
        high = jnp.dot(
            bottom[...], after[halo], precision=lax.Precision.HIGHEST, preferred_element_type=jnp.float32
        )
        for c in range(2):
            lanes = pl.ds(c * TILE, TILE)
            work[f, c, pl.ds(0, HALO)] += low[:, c * TILE : (c + 1) * TILE]
            work[f, c, pl.ds(ROWS - HALO, HALO)] += high[:, c * TILE : (c + 1) * TILE]
            copy = pltpu.make_async_copy(work.at[f, c], out_hbm.at[f, :, lanes], sems.at[f, c])
            copy.start()
            copies.append(copy)
    for copy in copies:
        copy.wait()


def vmem_spec():
    return pl.BlockSpec(memory_space=pltpu.VMEM)


def any_spec():
    return pl.BlockSpec(memory_space=pl.ANY)


def pack(velocity):
    f32 = jnp.float32
    return pl.pallas_call(
        pack_kernel,
        out_shape=(
            pltpu.VMEM((FIELDS, 2, PAD, TILE), f32),
            pltpu.VMEM((FIELDS * HALO, LANES), f32),
            pltpu.VMEM((FIELDS * HALO, LANES), f32),
            pltpu.VMEM((FIELDS * BLOCKS * 4, TILE), f32),
            pltpu.VMEM((FIELDS * BLOCKS * 4, TILE), f32),
        ),
        in_specs=[any_spec()],
        out_specs=(vmem_spec(),) * 5,
        scratch_shapes=[pltpu.SemaphoreType.DMA((FIELDS, 2))],
        compiler_params=pltpu.CompilerParams(vmem_limit_bytes=16 * MIB),
        name="pack",
    )(pltpu.with_memory_space_constraint(velocity, pltpu.HBM))


def inner(pad):
    return pl.pallas_call(
        inner_kernel,
        out_shape=pltpu.VMEM((FIELDS, 2, ROWS, TILE), jnp.float32),
        in_specs=[vmem_spec()],
        out_specs=vmem_spec(),
        scratch_shapes=[pltpu.VMEM((4, (WARM + CHUNK + WARM) * SUB, TILE), jnp.float32)],
        compiler_params=pltpu.CompilerParams(vmem_limit_bytes=16 * MIB),
        cost_estimate=pl.CostEstimate(flops=10**9, bytes_accessed=12 * MIB, transcendentals=0),
        name="inner",
    )(pad)


def edges(partial, before, after, left, right):
    top, bottom = edge_matrices()
    return pl.pallas_call(
        edge_kernel,
        out_shape=jax.ShapeDtypeStruct((FIELDS, ROWS, LANES), jnp.float32),
        in_specs=[vmem_spec()] * 7,
        out_specs=any_spec(),
        scratch_shapes=[
            pltpu.VMEM((FIELDS, 2, ROWS, TILE), jnp.float32),
            pltpu.SemaphoreType.DMA((FIELDS, 2)),
        ],
        compiler_params=pltpu.CompilerParams(vmem_limit_bytes=24 * MIB),
        name="edges",
    )(pltpu.with_memory_space_constraint(partial, pltpu.VMEM), before, after, left, right, jnp.asarray(top), jnp.asarray(bottom))


def on_device(velocity):
    pad, head, tail, first, last = pack(velocity)
    size_x, size_z = lax.axis_size("gx"), lax.axis_size("gz")

    def shift(value, axis, size, by):
        return lax.ppermute(value, axis, [(i, (i + by) % size) for i in range(size)])

    left = shift(last, "gz", size_z, 1)
    right = shift(first, "gz", size_z, -1)
    before = shift(tail, "gx", size_x, 1)
    after = shift(head, "gx", size_x, -1)
    partial = inner(pltpu.with_memory_space_constraint(pad, pltpu.VMEM))
    return edges(partial, before, after, left, right)


def solution(mesh):
    return jax.shard_map(
        on_device,
        mesh=mesh,
        in_specs=(P(None, "gx", "gz"),),
        out_specs=P(None, "gx", "gz"),
        check_vma=False,
    )
```

```python
import math

import jax
import jax.numpy as jnp
import numpy as np
from jax import lax
from jax.experimental import pallas as pl
from jax.experimental.pallas import tpu as pltpu
from jax.sharding import PartitionSpec as P

FIELDS, ROWS, LANES = 4, 1536, 256
HALO = 24
PAD = 1576
SUB = 8
CHUNK = ROWS // SUB + 1
WARM = HALO - 2
STEPS = 216
UNROLL = 8
EARLY = 2
LONG = SUB * CHUNK
TILE = 128
BLOCKS = ROWS // TILE
RATIO = (math.sqrt(5.0) - 3.0) / 2.0
KAPPA = -1.0 / (3.0 * RATIO)
NEAR = 7.0 / 9.0 / KAPPA
FAR = 1.0 / 36.0 / KAPPA
MIB = 1 << 20


def edge_matrices():
    def green(m):
        return RATIO ** np.abs(m) / (KAPPA * (1.0 - RATIO * RATIO))

    def weight(m):
        return 7.0 / 9.0 * (green(m + 1) - green(m - 1)) + 1.0 / 36.0 * (green(m + 2) - green(m - 2))

    here = np.arange(HALO)[:, None]
    there = np.arange(HALO)[None, :]
    top = weight(here - (there - HALO))
    bottom = weight(here - (there + HALO))
    return top.astype(np.float32), bottom.astype(np.float32)


def difference_matrix():
    gap = lax.broadcasted_iota(jnp.int32, (LANES, LANES), 0) - lax.broadcasted_iota(
        jnp.int32, (LANES, LANES), 1
    )
    size = jnp.abs(gap)
    weight = jnp.where(size == 1, 45.0, jnp.where(size == 2, -9.0, jnp.where(size == 3, 1.0, 0.0)))
    return jnp.where(gap < 0, -weight, weight).astype(jnp.bfloat16)


def spanwise(here, matrix):
    high = here.astype(jnp.bfloat16)
    rest = here - high.astype(jnp.float32)
    middle = rest.astype(jnp.bfloat16)
    low = (rest - middle.astype(jnp.float32)).astype(jnp.bfloat16)
    total = jnp.dot(high, matrix, preferred_element_type=jnp.float32)
    total += jnp.dot(middle, matrix, preferred_element_type=jnp.float32)
    total += jnp.dot(low, matrix, preferred_element_type=jnp.float32)
    return total * (1.0 / 60.0)


def field_rows(pad, f, row, count):
    rows = pl.ds(HALO + row, count)
    return jnp.concatenate([pad[f, 0, rows], pad[f, 1, rows]], axis=1)


def is_even(axis):
    return lax.rem(lax.axis_index(axis), 2) == 0


def pack_kernel(v_hbm, pad, z_part, near_x, far_x, near_z, far_z, sems):
    copies = []
    for f in range(FIELDS):
        for c in range(2):
            lanes = pl.ds(c * TILE, TILE)
            copy = pltpu.make_async_copy(v_hbm.at[f, :, lanes], pad.at[f, c, pl.ds(HALO, ROWS)], sems.at[f, c])
            copy.start()
            copies.append(copy)
    even_x, even_z = is_even("gx"), is_even("gz")
    matrix = difference_matrix()
    zeros = jnp.zeros((HALO, TILE), jnp.float32)
    for f in range(FIELDS):
        for c in range(2):
            pad[f, c, pl.ds(0, HALO)] = zeros
            pad[f, c, pl.ds(HALO + ROWS, PAD - HALO - ROWS)] = jnp.zeros((PAD - HALO - ROWS, TILE), jnp.float32)
    lane = lax.broadcasted_iota(jnp.int32, (TILE, TILE), 1)
    for f in range(FIELDS):
        for c in range(2):
            copies[2 * f + c].wait()
        for c in range(2):
            at, lanes = pl.ds(f * HALO, HALO), pl.ds(c * TILE, TILE)
            head, tail = pad[f, c, pl.ds(HALO, HALO)], pad[f, c, pl.ds(ROWS, HALO)]
            near_x[at, lanes] = jnp.where(even_x, tail, head)
            far_x[at, lanes] = jnp.where(even_x, head, tail)
        for b in range(BLOCKS):
            rows = pl.ds(HALO + b * TILE, TILE)
            turned = jnp.where(lane < 64, pad[f, 0, rows], pad[f, 1, rows]).T
            at = pl.ds((f * BLOCKS + b) * 4, 4)
            first, last = turned[0:4], turned[TILE - 4 :]
            near_z[at] = jnp.where(even_z, last, first)
            far_z[at] = jnp.where(even_z, first, last)
        if f < EARLY:
            for b in range(0, ROWS, 256):
                total = spanwise(field_rows(pad, f, b, 256), matrix)
                z_part[f, 0, pl.ds(b, 256)] = total[:, :TILE]
                z_part[f, 1, pl.ds(b, 256)] = total[:, TILE:]


def inner_kernel(pad, z_part, out, swept):
    chains = [(f, c) for f in range(FIELDS) for c in (0, 1)]
    count = len(chains)

    def row(chain, k):
        f, c = chain
        return pad[f, c, pl.ds(k, SUB, stride=CHUNK)]

    def forward(step, carry):
        carry = list(carry)
        for u in range(UNROLL):
            k = step * UNROLL + u
            for n, chain in enumerate(chains):
                back2, back1, here, ahead1, y = carry[n]
                ahead2 = row(chain, k + 4)
                y = RATIO * y + (NEAR * (ahead1 - back1) + FAR * (ahead2 - back2))
                swept[n, pl.ds(pl.multiple_of(k * SUB, SUB), SUB)] = y
                carry[n] = (back1, here, ahead1, ahead2, y)
        return tuple(carry)

    zero = jnp.zeros((SUB, TILE), jnp.float32)
    start = tuple(tuple(row(chain, j) for j in range(4)) + (zero,) for chain in chains)
    lax.fori_loop(0, STEPS // UNROLL, forward, start)

    def value(n, k):
        return swept[n, pl.ds(pl.multiple_of(k * SUB, SUB), SUB)]

    carry = [zero] * count
    for k in range(WARM - 1, -1, -1):
        carry = [RATIO * carry[n] + value(n, k + WARM) for n in range(count)]
    sub = lax.broadcasted_iota(jnp.int32, (SUB, TILE), 0)
    beyond = RATIO / (1.0 - RATIO * RATIO)
    carry = [
        jnp.where(sub == SUB - 1, beyond * value(n, WARM + CHUNK - 1), pltpu.roll(carry[n], SUB - 1, 0))
        for n in range(count)
    ]

    def back(carry, k):
        carry = [RATIO * carry[n] + value(n, k + WARM) for n in range(count)]
        for n, (f, c) in enumerate(chains):
            at = pl.ds(k, SUB, stride=CHUNK)
            out[f, c, at] = carry[n] + z_part[f, c, at] if f < EARLY else carry[n]
        return carry

    def backward(step, carry):
        for u in range(UNROLL):
            carry = back(carry, CHUNK - 2 - (step * UNROLL + u))
        return tuple(carry)

    lax.fori_loop(0, CHUNK // UNROLL, backward, tuple(back(carry, CHUNK - 1)))


def edge_kernel(pad, inner, near_x, far_x, near_z, far_z, top, bottom, out_hbm, work, sems):
    copies = []
    even_x, even_z = is_even("gx"), is_even("gz")
    matrix = difference_matrix()
    zeros = jnp.zeros((TILE - 8, TILE), jnp.float32)
    none = jnp.zeros((1, TILE), jnp.float32)
    lane = lax.broadcasted_iota(jnp.int32, (TILE, TILE), 1)
    for f in range(FIELDS):
        for b in range(BLOCKS):
            rows = pl.ds(b * TILE, TILE)
            at = pl.ds((f * BLOCKS + b) * 4, 4)
            near, far = near_z[at], far_z[at]
            left, right = jnp.where(even_z, far, near), jnp.where(even_z, near, far)
            l3, l2, l1 = (left[n : n + 1] for n in (1, 2, 3))
            r1, r2, r3 = (right[n : n + 1] for n in (0, 1, 2))
            low = jnp.concatenate(
                [
                    -0.75 * l1 + 0.15 * l2 - l3 * (1.0 / 60.0),
                    0.15 * l1 - l2 * (1.0 / 60.0),
                    l1 * (-1.0 / 60.0),
                    none,
                ]
            )
            high = jnp.concatenate(
                [
                    none,
                    r1 * (1.0 / 60.0),
                    -0.15 * r1 + r2 * (1.0 / 60.0),
                    0.75 * r1 - 0.15 * r2 + r3 * (1.0 / 60.0),
                ]
            )
            turned = jnp.concatenate([low, zeros, high]).T
            parts = [inner[f, c, rows] for c in range(2)]
            if f >= EARLY:
                total = spanwise(field_rows(pad, f, b * TILE, TILE), matrix)
                parts = [parts[c] + total[:, c * TILE : (c + 1) * TILE] for c in range(2)]
            work[f, 0, rows] = parts[0] + jnp.where(lane < 64, turned, 0.0)
            work[f, 1, rows] = parts[1] + jnp.where(lane < 64, 0.0, turned)
        halo = pl.ds(f * HALO, HALO)
        near, far = near_x[halo], far_x[halo]
        before, after = jnp.where(even_x, far, near), jnp.where(even_x, near, far)
        low = jnp.dot(top[...], before, precision=lax.Precision.HIGHEST, preferred_element_type=jnp.float32)
        high = jnp.dot(bottom[...], after, precision=lax.Precision.HIGHEST, preferred_element_type=jnp.float32)
        for c in range(2):
            lanes = pl.ds(c * TILE, TILE)
            work[f, c, pl.ds(0, HALO)] += low[:, c * TILE : (c + 1) * TILE]
            work[f, c, pl.ds(ROWS - HALO, HALO)] += high[:, c * TILE : (c + 1) * TILE]
            copy = pltpu.make_async_copy(work.at[f, c], out_hbm.at[f, :, lanes], sems.at[f, c])
            copy.start()
            copies.append(copy)
    for copy in copies:
        copy.wait()


def vmem_spec():
    return pl.BlockSpec(memory_space=pltpu.VMEM)


def any_spec():
    return pl.BlockSpec(memory_space=pl.ANY)


def in_vmem(value):
    return pltpu.with_memory_space_constraint(value, pltpu.VMEM)


def pack(velocity):
    f32 = jnp.float32
    return pl.pallas_call(
        pack_kernel,
        out_shape=(
            pltpu.VMEM((FIELDS, 2, PAD, TILE), f32),
            pltpu.VMEM((EARLY, 2, LONG, TILE), f32),
            pltpu.VMEM((FIELDS * HALO, LANES), f32),
            pltpu.VMEM((FIELDS * HALO, LANES), f32),
            pltpu.VMEM((FIELDS * BLOCKS * 4, TILE), f32),
            pltpu.VMEM((FIELDS * BLOCKS * 4, TILE), f32),
        ),
        in_specs=[any_spec()],
        out_specs=(vmem_spec(),) * 6,
        scratch_shapes=[pltpu.SemaphoreType.DMA((FIELDS, 2))],
        compiler_params=pltpu.CompilerParams(vmem_limit_bytes=16 * MIB),
        name="pack",
    )(pltpu.with_memory_space_constraint(velocity, pltpu.HBM))


def inner(pad, z_part):
    return pl.pallas_call(
        inner_kernel,
        out_shape=pltpu.VMEM((FIELDS, 2, LONG, TILE), jnp.float32),
        in_specs=[vmem_spec()] * 2,
        out_specs=vmem_spec(),
        scratch_shapes=[pltpu.VMEM((2 * FIELDS, STEPS * SUB, TILE), jnp.float32)],
        compiler_params=pltpu.CompilerParams(vmem_limit_bytes=16 * MIB),
        cost_estimate=pl.CostEstimate(flops=10**9, bytes_accessed=12 * MIB, transcendentals=0),
        name="inner",
    )(in_vmem(pad), in_vmem(z_part))


def edges(pad, partial, near_x, far_x, near_z, far_z):
    top, bottom = edge_matrices()
    return pl.pallas_call(
        edge_kernel,
        out_shape=jax.ShapeDtypeStruct((FIELDS, ROWS, LANES), jnp.float32),
        in_specs=[vmem_spec()] * 8,
        out_specs=any_spec(),
        scratch_shapes=[
            pltpu.VMEM((FIELDS, 2, ROWS, TILE), jnp.float32),
            pltpu.SemaphoreType.DMA((FIELDS, 2)),
        ],
        compiler_params=pltpu.CompilerParams(vmem_limit_bytes=16 * MIB),
        name="edges",
    )(in_vmem(pad), in_vmem(partial), near_x, far_x, near_z, far_z, jnp.asarray(top), jnp.asarray(bottom))


def on_device(velocity):
    pad, z_part, near_x, far_x, near_z, far_z = pack(velocity)

    def swap(value, axis, first):
        size = lax.axis_size(axis)
        pairs = [(i % size, (i + 1) % size) for i in range(first, size, 2)]
        return lax.ppermute(value, axis, pairs + [(j, i) for i, j in pairs])

    near_z, far_z = swap(near_z, "gz", 0), swap(far_z, "gz", 1)
    near_x, far_x = swap(near_x, "gx", 0), swap(far_x, "gx", 1)
    partial = inner(pad, z_part)
    return edges(pad, partial, near_x, far_x, near_z, far_z)


def solution(mesh):
    return jax.shard_map(
        on_device,
        mesh=mesh,
        in_specs=(P(None, "gx", "gz"),),
        out_specs=P(None, "gx", "gz"),
        check_vma=False,
    )
```

```python
import math

import jax
import jax.numpy as jnp
import numpy as np
from jax import lax
from jax.experimental import pallas as pl
from jax.experimental.pallas import tpu as pltpu
from jax.sharding import PartitionSpec as P

FIELDS, ROWS, LANES = 4, 1536, 256
HALO = 24
PAD = 1576
SUB = 8
CHUNK = ROWS // SUB + 1
WARM = HALO - 2
STEPS = 216
UNROLL = 8
EARLY = 1
MIDDLE = 2
LONG = SUB * CHUNK
TILE = 128
BLOCKS = ROWS // TILE
TILE_ROWS = FIELDS * BLOCKS
RATIO = (math.sqrt(5.0) - 3.0) / 2.0
KAPPA = -1.0 / (3.0 * RATIO)
NEAR = 7.0 / 9.0 / KAPPA
FAR = 1.0 / 36.0 / KAPPA
MIB = 1 << 20


GAP = TILE_ROWS + 1
EDGE = 152
SCALE = 1.0 / (KAPPA * (1.0 - RATIO * RATIO))
TAIL = SCALE * (7.0 / 9.0 * (RATIO - 1.0 / RATIO) + 1.0 / 36.0 * (RATIO**2 - RATIO**-2))
NEXT = -1.0 / 12.0


def powers(exponent):
    value = jnp.where(exponent % 2 == 1, RATIO, 1.0)
    for bit in (2, 4, 8, 16):
        value = value * jnp.where((exponent // bit) % 2 == 1, RATIO**bit, 1.0)
    return value


def difference_matrix():
    gap = lax.broadcasted_iota(jnp.int32, (LANES, LANES), 0) - lax.broadcasted_iota(
        jnp.int32, (LANES, LANES), 1
    )
    size = jnp.abs(gap)
    weight = jnp.where(size == 1, 45.0, jnp.where(size == 2, -9.0, jnp.where(size == 3, 1.0, 0.0)))
    return jnp.where(gap < 0, -weight, weight).astype(jnp.bfloat16)


def spanwise(here, matrix):
    high = here.astype(jnp.bfloat16)
    rest = here - high.astype(jnp.float32)
    middle = rest.astype(jnp.bfloat16)
    low = (rest - middle.astype(jnp.float32)).astype(jnp.bfloat16)
    total = jnp.dot(high, matrix, preferred_element_type=jnp.float32)
    total += jnp.dot(middle, matrix, preferred_element_type=jnp.float32)
    total += jnp.dot(low, matrix, preferred_element_type=jnp.float32)
    return total * (1.0 / 60.0)


def field_rows(pad, f, row, count):
    rows = pl.ds(HALO + row, count)
    return jnp.concatenate([pad[f, 0, rows], pad[f, 1, rows]], axis=1)


def is_even(axis):
    return lax.rem(lax.axis_index(axis), 2) == 0


def pack_kernel(v_hbm, pad, z_part, near_x, far_x, near_z, far_z, turned_first, turned_last, sems):
    copies = []
    for f in range(FIELDS):
        for c in range(2):
            lanes = pl.ds(c * TILE, TILE)
            copy = pltpu.make_async_copy(v_hbm.at[f, :, lanes], pad.at[f, c, pl.ds(HALO, ROWS)], sems.at[f, c])
            copy.start()
            copies.append(copy)
    even_x, even_z = is_even("gx"), is_even("gz")
    matrix = difference_matrix()
    zeros = jnp.zeros((HALO, TILE), jnp.float32)
    for f in range(FIELDS):
        for c in range(2):
            pad[f, c, pl.ds(0, HALO)] = zeros
            pad[f, c, pl.ds(HALO + ROWS, PAD - HALO - ROWS)] = jnp.zeros((PAD - HALO - ROWS, TILE), jnp.float32)
    lane = lax.broadcasted_iota(jnp.int32, (TILE, TILE), 1)
    place = lax.broadcasted_iota(jnp.int32, (HALO, TILE), 0)
    head_weight, tail_weight = powers(place + 1), powers(HALO - place)
    for f in range(FIELDS):
        for c in range(2):
            copies[2 * f + c].wait()
        for c in range(2):
            lanes = pl.ds(c * TILE, TILE)
            head, tail = pad[f, c, pl.ds(HALO, HALO)], pad[f, c, pl.ds(ROWS, HALO)]
            head_sum = jnp.sum(head * head_weight, axis=0, keepdims=True)
            tail_sum = jnp.sum(tail * tail_weight, axis=0, keepdims=True)
            near_x[pl.ds(2 * f, 1), lanes] = jnp.where(even_x, tail_sum, head_sum)
            far_x[pl.ds(2 * f, 1), lanes] = jnp.where(even_x, head_sum, tail_sum)
            near_x[pl.ds(2 * f + 1, 1), lanes] = jnp.where(even_x, tail[HALO - 1 :], head[:1])
            far_x[pl.ds(2 * f + 1, 1), lanes] = jnp.where(even_x, head[:1], tail[HALO - 1 :])
        for b in range(BLOCKS):
            rows = pl.ds(HALO + b * TILE, TILE)
            turned = jnp.where(lane < 64, pad[f, 0, rows], pad[f, 1, rows]).T
            block = f * BLOCKS + b
            turned_first[pl.ds(block, SUB, stride=GAP)] = turned[:SUB]
            turned_last[pl.ds(block + 3, SUB, stride=GAP)] = turned[TILE - SUB :]
        if f < EARLY:
            for b in range(0, ROWS, 256):
                total = spanwise(field_rows(pad, f, b, 256), matrix)
                z_part[f, 0, pl.ds(b, 256)] = total[:, :TILE]
                z_part[f, 1, pl.ds(b, 256)] = total[:, TILE:]
    first, last = turned_first[0:EDGE], turned_last[5 * GAP + 3 : 5 * GAP + 3 + EDGE]
    near_z[...] = jnp.where(even_z, last, first)
    far_z[...] = jnp.where(even_z, first, last)


def inner_body(pad, z_part, out, swept):
    chains = [(f, c) for f in range(FIELDS) for c in (0, 1)]
    count = len(chains)

    def row(chain, k):
        f, c = chain
        return pad[f, c, pl.ds(k, SUB, stride=CHUNK)]

    def forward(step, carry):
        carry = list(carry)
        for u in range(UNROLL):
            k = step * UNROLL + u
            for n, chain in enumerate(chains):
                back2, back1, here, ahead1, y = carry[n]
                ahead2 = row(chain, k + 4)
                y = RATIO * y + (NEAR * (ahead1 - back1) + FAR * (ahead2 - back2))
                swept[n, pl.ds(pl.multiple_of(k * SUB, SUB), SUB)] = y
                carry[n] = (back1, here, ahead1, ahead2, y)
        return tuple(carry)

    zero = jnp.zeros((SUB, TILE), jnp.float32)
    start = tuple(tuple(row(chain, j) for j in range(4)) + (zero,) for chain in chains)
    lax.fori_loop(0, STEPS // UNROLL, forward, start)

    def value(n, k):
        return swept[n, pl.ds(pl.multiple_of(k * SUB, SUB), SUB)]

    carry = [zero] * count
    for k in range(WARM - 1, -1, -1):
        carry = [RATIO * carry[n] + value(n, k + WARM) for n in range(count)]
    sub = lax.broadcasted_iota(jnp.int32, (SUB, TILE), 0)
    beyond = RATIO / (1.0 - RATIO * RATIO)
    carry = [
        jnp.where(sub == SUB - 1, beyond * value(n, WARM + CHUNK - 1), pltpu.roll(carry[n], SUB - 1, 0))
        for n in range(count)
    ]

    def back(carry, k):
        carry = [RATIO * carry[n] + value(n, k + WARM) for n in range(count)]
        for n, (f, c) in enumerate(chains):
            at = pl.ds(k, SUB, stride=CHUNK)
            out[f, c, at] = carry[n] + z_part[f, c, at] if f < EARLY else carry[n]
        return carry

    def backward(step, carry):
        for u in range(UNROLL):
            carry = back(carry, CHUNK - 2 - (step * UNROLL + u))
        return tuple(carry)

    lax.fori_loop(0, CHUNK // UNROLL, backward, tuple(back(carry, CHUNK - 1)))
    matrix = difference_matrix()
    for f in range(EARLY, MIDDLE):
        for b in range(0, ROWS, 256):
            total = spanwise(field_rows(pad, f, b, 256), matrix)
            out[f, 0, pl.ds(b, 256)] += total[:, :TILE]
            out[f, 1, pl.ds(b, 256)] += total[:, TILE:]


def waits_longest():
    return lax.axis_index("gz") == 0


def first_kernel(pad, z_part, far_z_in, near_x_in, far_x_in, out, far_z, near_x, far_x, swept):
    pl.when(waits_longest())(lambda: inner_body(pad, z_part, out, swept))


def inner_kernel(pad, z_part, done, out, swept):
    pl.when(jnp.logical_not(waits_longest()))(lambda: inner_body(pad, z_part, out, swept))


def edge_kernel(pad, inner, far_z, near_z, far_x, near_x, out_hbm, work, turned_in, turned_out, sems):
    copies = []
    even_x, even_z = is_even("gx"), is_even("gz")
    matrix = difference_matrix()
    near, far = near_z[...], far_z[...]
    turned_in[0:EDGE] = jnp.where(even_z, far, near)
    turned_in[EDGE:] = jnp.where(even_z, near, far)
    l3, l2, l1 = (turned_in[n * GAP : n * GAP + TILE_ROWS] for n in range(3))
    r1, r2, r3 = (turned_in[EDGE + n * GAP : EDGE + n * GAP + TILE_ROWS] for n in range(3))
    none = jnp.zeros((TILE_ROWS, TILE), jnp.float32)
    for n, value in enumerate(
        (
            -0.75 * l1 + 0.15 * l2 - l3 * (1.0 / 60.0),
            0.15 * l1 - l2 * (1.0 / 60.0),
            l1 * (-1.0 / 60.0),
            none,
            none,
            r1 * (1.0 / 60.0),
            -0.15 * r1 + r2 * (1.0 / 60.0),
            0.75 * r1 - 0.15 * r2 + r3 * (1.0 / 60.0),
        )
    ):
        turned_out[n * GAP : n * GAP + TILE_ROWS] = value
    before, after = jnp.where(even_x, far_x[...], near_x[...]), jnp.where(even_x, near_x[...], far_x[...])
    place = lax.broadcasted_iota(jnp.int32, (HALO, TILE), 0)
    top, bottom = TAIL * powers(place), TAIL * powers(HALO - 1 - place)
    top_next, bottom_next = jnp.where(place == 0, NEXT, 0.0), jnp.where(place == HALO - 1, NEXT, 0.0)
    zeros = jnp.zeros((TILE - 2 * SUB, TILE), jnp.float32)
    lane = lax.broadcasted_iota(jnp.int32, (TILE, TILE), 1)
    for f in range(FIELDS):
        for b in range(BLOCKS):
            rows = pl.ds(b * TILE, TILE)
            columns = turned_out[pl.ds(f * BLOCKS + b, SUB, stride=GAP)]
            turned = jnp.concatenate([columns, zeros, columns]).T
            parts = [inner[f, c, rows] for c in range(2)]
            if f >= MIDDLE:
                total = spanwise(field_rows(pad, f, b * TILE, TILE), matrix)
                parts = [parts[c] + total[:, c * TILE : (c + 1) * TILE] for c in range(2)]
            work[f, 0, rows] = parts[0] + jnp.where(lane < 4, turned, 0.0)
            work[f, 1, rows] = parts[1] + jnp.where(lane < TILE - 4, 0.0, turned)
        for c in range(2):
            lanes = slice(c * TILE, (c + 1) * TILE)
            work[f, c, pl.ds(0, HALO)] += (
                top * before[2 * f : 2 * f + 1, lanes] + top_next * before[2 * f + 1 : 2 * f + 2, lanes]
            )
            work[f, c, pl.ds(ROWS - HALO, HALO)] -= (
                bottom * after[2 * f : 2 * f + 1, lanes] + bottom_next * after[2 * f + 1 : 2 * f + 2, lanes]
            )
            copy = pltpu.make_async_copy(work.at[f, c], out_hbm.at[f, :, pl.ds(c * TILE, TILE)], sems.at[f, c])
            copy.start()
            copies.append(copy)
    for copy in copies:
        copy.wait()


def vmem_spec():
    return pl.BlockSpec(memory_space=pltpu.VMEM)


def any_spec():
    return pl.BlockSpec(memory_space=pl.ANY)


def in_vmem(value):
    return pltpu.with_memory_space_constraint(value, pltpu.VMEM)


def call(kernel, outs, scratch, ins, name, aliases=None, out_specs=None):
    return pl.pallas_call(
        kernel,
        out_shape=outs,
        in_specs=[any_spec() if name == "pack" else vmem_spec() for _ in ins],
        out_specs=out_specs or (vmem_spec(),) * len(outs),
        scratch_shapes=scratch,
        input_output_aliases=aliases or {},
        compiler_params=pltpu.CompilerParams(vmem_limit_bytes=16 * MIB),
        name=name,
    )(*ins)


def on_device(velocity):
    f32 = jnp.float32
    block = pltpu.VMEM((FIELDS, 2, LONG, TILE), f32)
    x_edge, z_edge = pltpu.VMEM((2 * FIELDS, LANES), f32), pltpu.VMEM((EDGE, TILE), f32)
    turned = pltpu.VMEM((400, TILE), f32)
    sems = pltpu.SemaphoreType.DMA((FIELDS, 2))
    swept = [pltpu.VMEM((2 * FIELDS, STEPS * SUB, TILE), f32)]
    pad, z_part, near_x, far_x, near_z, far_z = call(
        pack_kernel,
        (
            pltpu.VMEM((FIELDS, 2, PAD, TILE), f32),
            pltpu.VMEM((EARLY, 2, LONG, TILE), f32),
            x_edge,
            x_edge,
            z_edge,
            z_edge,
        ),
        [turned, turned, sems],
        [pltpu.with_memory_space_constraint(velocity, pltpu.HBM)],
        "pack",
    )

    def swap(value, axis, first):
        size = lax.axis_size(axis)
        pairs = [(i % size, (i + 1) % size) for i in range(first, size, 2)]
        return lax.ppermute(value, axis, pairs + [(j, i) for i, j in pairs])

    pad, z_part = in_vmem(pad), in_vmem(z_part)
    near_z = swap(near_z, "gz", 0)
    partial, far_z, near_x, far_x = call(
        first_kernel,
        (block, z_edge, x_edge, x_edge),
        swept,
        [pad, z_part, in_vmem(far_z), in_vmem(near_x), in_vmem(far_x)],
        "first",
        {2: 1, 3: 2, 4: 3},
    )
    far_z = swap(far_z, "gz", 1)
    near_x, far_x = swap(near_x, "gx", 0), swap(far_x, "gx", 1)
    (partial,) = call(inner_kernel, (block,), swept, [pad, z_part, in_vmem(partial)], "inner", {2: 0})
    return call(
        edge_kernel,
        jax.ShapeDtypeStruct((FIELDS, ROWS, LANES), f32),
        [pltpu.VMEM((FIELDS, 2, ROWS, TILE), f32), pltpu.VMEM((2 * EDGE, TILE), f32), turned, sems],
        [pad, in_vmem(partial), far_z, near_z, far_x, near_x],
        "edges",
        None,
        any_spec(),
    )


def solution(mesh):
    return jax.shard_map(
        on_device,
        mesh=mesh,
        in_specs=(P(None, "gx", "gz"),),
        out_specs=P(None, "gx", "gz"),
        check_vma=False,
    )
```

```python
import math

import jax
import jax.numpy as jnp
import numpy as np
from jax import lax
from jax.experimental import pallas as pl
from jax.experimental.pallas import tpu as pltpu
from jax.sharding import PartitionSpec as P

FIELDS, ROWS, LANES = 4, 1536, 256
HALO = 24
PAD = 1576
SUB = 8
CHUNK = ROWS // SUB + 1
WARM = HALO - 2
STEPS = 216
UNROLL = 8
EARLY = 1
MIDDLE = 2
LONG = SUB * CHUNK
TILE = 128
BLOCKS = ROWS // TILE
TILE_ROWS = FIELDS * BLOCKS
RATIO = (math.sqrt(5.0) - 3.0) / 2.0
KAPPA = -1.0 / (3.0 * RATIO)
NEAR = 7.0 / 9.0 / KAPPA
FAR = 1.0 / 36.0 / KAPPA
MIB = 1 << 20


GAP = TILE_ROWS + 1
EDGE = 152
SCALE = 1.0 / (KAPPA * (1.0 - RATIO * RATIO))
TAIL = SCALE * (7.0 / 9.0 * (RATIO - 1.0 / RATIO) + 1.0 / 36.0 * (RATIO**2 - RATIO**-2))
NEXT = -1.0 / 12.0


def powers(exponent):
    value = jnp.where(exponent % 2 == 1, RATIO, 1.0)
    for bit in (2, 4, 8, 16):
        value = value * jnp.where((exponent // bit) % 2 == 1, RATIO**bit, 1.0)
    return value


def difference_matrix():
    gap = lax.broadcasted_iota(jnp.int32, (LANES, LANES), 0) - lax.broadcasted_iota(
        jnp.int32, (LANES, LANES), 1
    )
    size = jnp.abs(gap)
    weight = jnp.where(size == 1, 45.0, jnp.where(size == 2, -9.0, jnp.where(size == 3, 1.0, 0.0)))
    return jnp.where(gap < 0, -weight, weight).astype(jnp.bfloat16)


def spanwise(here, matrix):
    high = here.astype(jnp.bfloat16)
    rest = here - high.astype(jnp.float32)
    middle = rest.astype(jnp.bfloat16)
    low = (rest - middle.astype(jnp.float32)).astype(jnp.bfloat16)
    total = jnp.dot(high, matrix, preferred_element_type=jnp.float32)
    total += jnp.dot(middle, matrix, preferred_element_type=jnp.float32)
    total += jnp.dot(low, matrix, preferred_element_type=jnp.float32)
    return total * (1.0 / 60.0)


def field_rows(pad, f, row, count):
    rows = pl.ds(HALO + row, count)
    return jnp.concatenate([pad[f, 0, rows], pad[f, 1, rows]], axis=1)


def is_even(axis):
    return lax.rem(lax.axis_index(axis), 2) == 0


def pack_kernel(v_hbm, pad, z_part, near_x, far_x, near_x_too, far_x_too, near_z, far_z, turned_first, turned_last, sems):
    copies = []
    for f in range(FIELDS):
        for c in range(2):
            lanes = pl.ds(c * TILE, TILE)
            copy = pltpu.make_async_copy(v_hbm.at[f, :, lanes], pad.at[f, c, pl.ds(HALO, ROWS)], sems.at[f, c])
            copy.start()
            copies.append(copy)
    even_x, even_z = is_even("gx"), is_even("gz")
    matrix = difference_matrix()
    zeros = jnp.zeros((HALO, TILE), jnp.float32)
    for f in range(FIELDS):
        for c in range(2):
            pad[f, c, pl.ds(0, HALO)] = zeros
            pad[f, c, pl.ds(HALO + ROWS, PAD - HALO - ROWS)] = jnp.zeros((PAD - HALO - ROWS, TILE), jnp.float32)
    lane = lax.broadcasted_iota(jnp.int32, (TILE, TILE), 1)
    place = lax.broadcasted_iota(jnp.int32, (HALO, TILE), 0)
    head_weight, tail_weight = powers(place + 1), powers(HALO - place)
    for f in range(FIELDS):
        for c in range(2):
            copies[2 * f + c].wait()
        for c in range(2):
            lanes = pl.ds(c * TILE, TILE)
            head, tail = pad[f, c, pl.ds(HALO, HALO)], pad[f, c, pl.ds(ROWS, HALO)]
            head_sum = jnp.sum(head * head_weight, axis=0, keepdims=True)
            tail_sum = jnp.sum(tail * tail_weight, axis=0, keepdims=True)
            near_x[pl.ds(2 * f, 1), lanes] = jnp.where(even_x, tail_sum, head_sum)
            far_x[pl.ds(2 * f, 1), lanes] = jnp.where(even_x, head_sum, tail_sum)
            near_x[pl.ds(2 * f + 1, 1), lanes] = jnp.where(even_x, tail[HALO - 1 :], head[:1])
            far_x[pl.ds(2 * f + 1, 1), lanes] = jnp.where(even_x, head[:1], tail[HALO - 1 :])
        for b in range(BLOCKS):
            rows = pl.ds(HALO + b * TILE, TILE)
            turned = jnp.where(lane < 64, pad[f, 0, rows], pad[f, 1, rows]).T
            block = f * BLOCKS + b
            turned_first[pl.ds(block, SUB, stride=GAP)] = turned[:SUB]
            turned_last[pl.ds(block + 3, SUB, stride=GAP)] = turned[TILE - SUB :]
        if f < EARLY:
            for b in range(0, ROWS, 256):
                total = spanwise(field_rows(pad, f, b, 256), matrix)
                z_part[f, 0, pl.ds(b, 256)] = total[:, :TILE]
                z_part[f, 1, pl.ds(b, 256)] = total[:, TILE:]
    first, last = turned_first[0:EDGE], turned_last[5 * GAP + 3 : 5 * GAP + 3 + EDGE]
    near_x_too[...] = near_x[...]
    far_x_too[...] = far_x[...]
    near_z[...] = jnp.where(even_z, last, first)
    far_z[...] = jnp.where(even_z, first, last)


def inner_body(pad, z_part, out, swept):
    chains = [(f, c) for f in range(FIELDS) for c in (0, 1)]
    count = len(chains)

    def row(chain, k):
        f, c = chain
        return pad[f, c, pl.ds(k, SUB, stride=CHUNK)]

    def forward(step, carry):
        carry = list(carry)
        for u in range(UNROLL):
            k = step * UNROLL + u
            for n, chain in enumerate(chains):
                back2, back1, here, ahead1, y = carry[n]
                ahead2 = row(chain, k + 4)
                y = RATIO * y + (NEAR * (ahead1 - back1) + FAR * (ahead2 - back2))
                swept[n, pl.ds(pl.multiple_of(k * SUB, SUB), SUB)] = y
                carry[n] = (back1, here, ahead1, ahead2, y)
        return tuple(carry)

    zero = jnp.zeros((SUB, TILE), jnp.float32)
    start = tuple(tuple(row(chain, j) for j in range(4)) + (zero,) for chain in chains)
    lax.fori_loop(0, STEPS // UNROLL, forward, start)

    def value(n, k):
        return swept[n, pl.ds(pl.multiple_of(k * SUB, SUB), SUB)]

    carry = [zero] * count
    for k in range(WARM - 1, -1, -1):
        carry = [RATIO * carry[n] + value(n, k + WARM) for n in range(count)]
    sub = lax.broadcasted_iota(jnp.int32, (SUB, TILE), 0)
    beyond = RATIO / (1.0 - RATIO * RATIO)
    carry = [
        jnp.where(sub == SUB - 1, beyond * value(n, WARM + CHUNK - 1), pltpu.roll(carry[n], SUB - 1, 0))
        for n in range(count)
    ]

    def back(carry, k):
        carry = [RATIO * carry[n] + value(n, k + WARM) for n in range(count)]
        for n, (f, c) in enumerate(chains):
            at = pl.ds(k, SUB, stride=CHUNK)
            out[f, c, at] = carry[n] + z_part[f, c, at] if f < EARLY else carry[n]
        return carry

    def backward(step, carry):
        for u in range(UNROLL):
            carry = back(carry, CHUNK - 2 - (step * UNROLL + u))
        return tuple(carry)

    lax.fori_loop(0, CHUNK // UNROLL, backward, tuple(back(carry, CHUNK - 1)))
    matrix = difference_matrix()
    for f in range(EARLY, MIDDLE):
        for b in range(0, ROWS, 256):
            total = spanwise(field_rows(pad, f, b, 256), matrix)
            out[f, 0, pl.ds(b, 256)] += total[:, :TILE]
            out[f, 1, pl.ds(b, 256)] += total[:, TILE:]


def waits_longest():
    return lax.axis_index("gz") == 0


def first_kernel(pad, z_part, far_z_in, near_x_in, far_x_in, far_early, near_early, out, far_z, near_x, far_x, swept):
    pl.when(waits_longest())(lambda: inner_body(pad, z_part, out, swept))


def inner_kernel(pad, z_part, done, out, swept):
    pl.when(jnp.logical_not(waits_longest()))(lambda: inner_body(pad, z_part, out, swept))


def halo_columns(left, right, turned_in, turned_out):
    turned_in[0:EDGE] = left
    turned_in[EDGE:] = right
    l3, l2, l1 = (turned_in[n * GAP : n * GAP + TILE_ROWS] for n in range(3))
    r1, r2, r3 = (turned_in[EDGE + n * GAP : EDGE + n * GAP + TILE_ROWS] for n in range(3))
    none = jnp.zeros((TILE_ROWS, TILE), jnp.float32)
    for n, value in enumerate(
        (
            -0.75 * l1 + 0.15 * l2 - l3 * (1.0 / 60.0),
            0.15 * l1 - l2 * (1.0 / 60.0),
            l1 * (-1.0 / 60.0),
            none,
            none,
            r1 * (1.0 / 60.0),
            -0.15 * r1 + r2 * (1.0 / 60.0),
            0.75 * r1 - 0.15 * r2 + r3 * (1.0 / 60.0),
        )
    ):
        turned_out[n * GAP : n * GAP + TILE_ROWS] = value


def finish(sides, late, spare, pad, inner, before, after, out_hbm, work, turned_out, sems):
    copies = []
    matrix = difference_matrix()
    place = lax.broadcasted_iota(jnp.int32, (HALO, TILE), 0)
    top, bottom = TAIL * powers(place), TAIL * powers(HALO - 1 - place)
    top_next, bottom_next = jnp.where(place == 0, NEXT, 0.0), jnp.where(place == HALO - 1, NEXT, 0.0)
    zeros = jnp.zeros((TILE - 2 * SUB, TILE), jnp.float32)
    lane = lax.broadcasted_iota(jnp.int32, (TILE, TILE), 1)
    half = ROWS // 2
    for f in range(FIELDS):
        for h in range(2):
            for b in range(h * BLOCKS // 2, (h + 1) * BLOCKS // 2):
                rows = pl.ds(b * TILE, TILE)
                columns = turned_out[pl.ds(f * BLOCKS + b, SUB, stride=GAP)]
                turned = jnp.concatenate([columns, zeros, columns]).T
                parts = [inner[f, c, rows] for c in range(2)]
                if late and f >= MIDDLE:
                    total = spanwise(field_rows(pad, f, b * TILE, TILE), matrix)
                    parts = [parts[c] + total[:, c * TILE : (c + 1) * TILE] for c in range(2)]
                    if spare is not None:
                        spare[f, 0, rows] = parts[0]
                if 0 in sides:
                    work[f, 0, rows] = parts[0] + jnp.where(lane < 4, turned, 0.0)
                if 1 in sides:
                    work[f, 1, rows] = parts[1] + jnp.where(lane < TILE - 4, 0.0, turned)
            for c in sides:
                lanes = slice(c * TILE, (c + 1) * TILE)
                if h == 0:
                    work[f, c, pl.ds(0, HALO)] += (
                        top * before[2 * f : 2 * f + 1, lanes] + top_next * before[2 * f + 1 : 2 * f + 2, lanes]
                    )
                else:
                    work[f, c, pl.ds(ROWS - HALO, HALO)] -= (
                        bottom * after[2 * f : 2 * f + 1, lanes] + bottom_next * after[2 * f + 1 : 2 * f + 2, lanes]
                    )
                rows = pl.ds(h * half, half)
                copy = pltpu.make_async_copy(
                    work.at[f, c, rows], out_hbm.at[f, rows, pl.ds(c * TILE, TILE)], sems.at[f, c, h]
                )
                copy.start()
                copies.append(copy)
    for copy in copies:
        copy.wait()


def half_kernel(pad, inner_in, near_z, far_x, near_x, out_hbm, inner, work, turned_in, turned_out, sems):
    def body():
        even_x = is_even("gx")
        before = jnp.where(even_x, far_x[...], near_x[...])
        after = jnp.where(even_x, near_x[...], far_x[...])
        halo_columns(jnp.zeros((EDGE, TILE), jnp.float32), near_z[...], turned_in, turned_out)
        finish((1,), True, inner, pad, inner, before, after, out_hbm, work, turned_out, sems)

    pl.when(waits_longest())(body)


def edge_kernel(
    pad, inner, far_z, near_z, far_x, near_x, far_early, near_early, half, out_hbm, work, turned_in, turned_out, sems
):
    even_x, even_z = is_even("gx"), is_even("gz")
    far_x, near_x = far_x[...] + far_early[...], near_x[...] + near_early[...]
    before, after = jnp.where(even_x, far_x, near_x), jnp.where(even_x, near_x, far_x)
    left, right = jnp.where(even_z, far_z[...], near_z[...]), jnp.where(even_z, near_z[...], far_z[...])
    halo_columns(left, right, turned_in, turned_out)

    @pl.when(waits_longest())
    def _():
        finish((0,), False, None, pad, inner, before, after, out_hbm, work, turned_out, sems)

    @pl.when(jnp.logical_not(waits_longest()))
    def _():
        finish((0, 1), True, None, pad, inner, before, after, out_hbm, work, turned_out, sems)


def vmem_spec():
    return pl.BlockSpec(memory_space=pltpu.VMEM)


def any_spec():
    return pl.BlockSpec(memory_space=pl.ANY)


def in_vmem(value):
    return pltpu.with_memory_space_constraint(value, pltpu.VMEM)


def call(kernel, outs, scratch, ins, name, aliases=None, out_specs=None):
    return pl.pallas_call(
        kernel,
        out_shape=outs,
        in_specs=[any_spec() if value.ndim == 3 else vmem_spec() for value in ins],
        out_specs=out_specs or (vmem_spec(),) * len(outs),
        scratch_shapes=scratch,
        input_output_aliases=aliases or {},
        compiler_params=pltpu.CompilerParams(vmem_limit_bytes=16 * MIB),
        name=name,
    )(*ins)


def on_device(velocity):
    f32 = jnp.float32
    block = pltpu.VMEM((FIELDS, 2, LONG, TILE), f32)
    x_edge, z_edge = pltpu.VMEM((2 * FIELDS, LANES), f32), pltpu.VMEM((EDGE, TILE), f32)
    turned = pltpu.VMEM((400, TILE), f32)
    sems = pltpu.SemaphoreType.DMA((FIELDS, 2))
    swept = [pltpu.VMEM((2 * FIELDS, STEPS * SUB, TILE), f32)]
    pad, z_part, near_early, far_early, near_x, far_x, near_z, far_z = call(
        pack_kernel,
        (
            pltpu.VMEM((FIELDS, 2, PAD, TILE), f32),
            pltpu.VMEM((EARLY, 2, LONG, TILE), f32),
            x_edge,
            x_edge,
            x_edge,
            x_edge,
            z_edge,
            z_edge,
        ),
        [turned, turned, sems],
        [pltpu.with_memory_space_constraint(velocity, pltpu.HBM)],
        "pack",
    )

    size_x, size_z = lax.axis_size("gx"), lax.axis_size("gz")

    def swap_z(value, first):
        pairs = [(i % size_z, (i + 1) % size_z) for i in range(first, size_z, 2)]
        return lax.ppermute(value, "gz", pairs + [(j, i) for i, j in pairs])

    def swap_x(value, first, columns):
        pairs = [
            (i % size_x * size_z + k, (i + 1) % size_x * size_z + k) for i in range(first, size_x, 2) for k in columns
        ]
        return lax.ppermute(value, ("gx", "gz"), pairs + [(j, i) for i, j in pairs])

    pad, z_part = in_vmem(pad), in_vmem(z_part)
    early, others = range(1), range(1, size_z)
    far_early, near_early = swap_x(far_early, 1, early), swap_x(near_early, 0, early)
    near_z = swap_z(near_z, 0)
    partial, far_z, near_x, far_x = call(
        first_kernel,
        (block, z_edge, x_edge, x_edge),
        swept,
        [pad, z_part, in_vmem(far_z), in_vmem(near_x), in_vmem(far_x), far_early, near_early],
        "first",
        {2: 1, 3: 2, 4: 3},
    )
    far_z = swap_z(far_z, 1)
    far_x, near_x = swap_x(far_x, 1, others), swap_x(near_x, 0, others)
    (partial,) = call(inner_kernel, (block,), swept, [pad, z_part, in_vmem(partial)], "inner", {2: 0})
    work = [
        pltpu.VMEM((FIELDS, 2, ROWS, TILE), f32),
        pltpu.VMEM((2 * EDGE, TILE), f32),
        turned,
        pltpu.SemaphoreType.DMA((FIELDS, 2, 2)),
    ]
    whole = pltpu.HBM((FIELDS, ROWS, LANES), f32)
    half, partial = call(
        half_kernel,
        (whole, block),
        work,
        [pad, in_vmem(partial), near_z, far_early, near_early],
        "half",
        {1: 1},
        (any_spec(), vmem_spec()),
    )
    return call(
        edge_kernel,
        whole,
        work,
        [pad, in_vmem(partial), far_z, near_z, far_x, near_x, far_early, near_early, half],
        "edges",
        {8: 0},
        any_spec(),
    )


def solution(mesh):
    return jax.shard_map(
        on_device,
        mesh=mesh,
        in_specs=(P(None, "gx", "gz"),),
        out_specs=P(None, "gx", "gz"),
        check_vma=False,
    )
```

```python
import math

import jax
import jax.numpy as jnp
import numpy as np
from jax import lax
from jax.experimental import pallas as pl
from jax.experimental.pallas import tpu as pltpu
from jax.sharding import PartitionSpec as P

FIELDS, ROWS, LANES = 4, 1536, 256
HALO = 24
PAD = 1576
SUB = 8
CHUNK = ROWS // SUB + 1
WARM = HALO - 2
STEPS = 216
UNROLL = 8
EARLY = 1
MIDDLE = 4
LONG = SUB * CHUNK
TILE = 128
BLOCKS = ROWS // TILE
TILE_ROWS = FIELDS * BLOCKS
RATIO = (math.sqrt(5.0) - 3.0) / 2.0
KAPPA = -1.0 / (3.0 * RATIO)
NEAR = 7.0 / 9.0 / KAPPA
FAR = 1.0 / 36.0 / KAPPA
MIB = 1 << 20


GAP = TILE_ROWS + 1
EDGE = 152
SCALE = 1.0 / (KAPPA * (1.0 - RATIO * RATIO))
TAIL = SCALE * (7.0 / 9.0 * (RATIO - 1.0 / RATIO) + 1.0 / 36.0 * (RATIO**2 - RATIO**-2))
NEXT = -1.0 / 12.0


def powers(exponent):
    value = jnp.where(exponent % 2 == 1, RATIO, 1.0)
    for bit in (2, 4, 8, 16):
        value = value * jnp.where((exponent // bit) % 2 == 1, RATIO**bit, 1.0)
    return value


def difference_matrix():
    gap = lax.broadcasted_iota(jnp.int32, (LANES, LANES), 0) - lax.broadcasted_iota(
        jnp.int32, (LANES, LANES), 1
    )
    size = jnp.abs(gap)
    weight = jnp.where(size == 1, 45.0, jnp.where(size == 2, -9.0, jnp.where(size == 3, 1.0, 0.0)))
    return jnp.where(gap < 0, -weight, weight).astype(jnp.bfloat16)


def spanwise(here, matrix):
    high = here.astype(jnp.bfloat16)
    rest = here - high.astype(jnp.float32)
    middle = rest.astype(jnp.bfloat16)
    low = (rest - middle.astype(jnp.float32)).astype(jnp.bfloat16)
    total = jnp.dot(high, matrix, preferred_element_type=jnp.float32)
    total += jnp.dot(middle, matrix, preferred_element_type=jnp.float32)
    total += jnp.dot(low, matrix, preferred_element_type=jnp.float32)
    return total * (1.0 / 60.0)


def field_rows(pad, f, row, count):
    rows = pl.ds(HALO + row, count)
    return jnp.concatenate([pad[f, 0, rows], pad[f, 1, rows]], axis=1)


def is_even(axis):
    return lax.rem(lax.axis_index(axis), 2) == 0


def pack_kernel(v_hbm, pad, z_part, near_x, far_x, near_z, far_z, turned_first, turned_last, sems):
    copies = []
    for f in range(FIELDS):
        for c in range(2):
            lanes = pl.ds(c * TILE, TILE)
            copy = pltpu.make_async_copy(v_hbm.at[f, :, lanes], pad.at[f, c, pl.ds(HALO, ROWS)], sems.at[f, c])
            copy.start()
            copies.append(copy)
    even_x, even_z = is_even("gx"), is_even("gz")
    matrix = difference_matrix()
    zeros = jnp.zeros((HALO, TILE), jnp.float32)
    for f in range(FIELDS):
        for c in range(2):
            pad[f, c, pl.ds(0, HALO)] = zeros
            pad[f, c, pl.ds(HALO + ROWS, PAD - HALO - ROWS)] = jnp.zeros((PAD - HALO - ROWS, TILE), jnp.float32)
    lane = lax.broadcasted_iota(jnp.int32, (TILE, TILE), 1)
    place = lax.broadcasted_iota(jnp.int32, (HALO, TILE), 0)
    head_weight, tail_weight = powers(place + 1), powers(HALO - place)
    for f in range(FIELDS):
        for c in range(2):
            copies[2 * f + c].wait()
        for c in range(2):
            lanes = pl.ds(c * TILE, TILE)
            head, tail = pad[f, c, pl.ds(HALO, HALO)], pad[f, c, pl.ds(ROWS, HALO)]
            head_sum = jnp.sum(head * head_weight, axis=0, keepdims=True)
            tail_sum = jnp.sum(tail * tail_weight, axis=0, keepdims=True)
            near_x[pl.ds(2 * f, 1), lanes] = jnp.where(even_x, tail_sum, head_sum)
            far_x[pl.ds(2 * f, 1), lanes] = jnp.where(even_x, head_sum, tail_sum)
            near_x[pl.ds(2 * f + 1, 1), lanes] = jnp.where(even_x, tail[HALO - 1 :], head[:1])
            far_x[pl.ds(2 * f + 1, 1), lanes] = jnp.where(even_x, head[:1], tail[HALO - 1 :])
        for b in range(BLOCKS):
            rows = pl.ds(HALO + b * TILE, TILE)
            turned = jnp.where(lane < 64, pad[f, 0, rows], pad[f, 1, rows]).T
            block = f * BLOCKS + b
            turned_first[pl.ds(block, SUB, stride=GAP)] = turned[:SUB]
            turned_last[pl.ds(block + 3, SUB, stride=GAP)] = turned[TILE - SUB :]
        if f < EARLY:
            for b in range(0, ROWS, 256):
                total = spanwise(field_rows(pad, f, b, 256), matrix)
                z_part[f, 0, pl.ds(b, 256)] = total[:, :TILE]
                z_part[f, 1, pl.ds(b, 256)] = total[:, TILE:]
    first, last = turned_first[0:EDGE], turned_last[5 * GAP + 3 : 5 * GAP + 3 + EDGE]
    near_z[...] = jnp.where(even_z, last, first)
    far_z[...] = jnp.where(even_z, first, last)


def inner_body(pad, z_part, out, swept):
    chains = [(f, c) for f in range(FIELDS) for c in (0, 1)]
    count = len(chains)

    def row(chain, k):
        f, c = chain
        return pad[f, c, pl.ds(k, SUB, stride=CHUNK)]

    def forward(step, carry):
        carry = list(carry)
        for u in range(UNROLL):
            k = step * UNROLL + u
            for n, chain in enumerate(chains):
                back2, back1, here, ahead1, y = carry[n]
                ahead2 = row(chain, k + 4)
                y = RATIO * y + (NEAR * (ahead1 - back1) + FAR * (ahead2 - back2))
                swept[n, pl.ds(pl.multiple_of(k * SUB, SUB), SUB)] = y
                carry[n] = (back1, here, ahead1, ahead2, y)
        return tuple(carry)

    zero = jnp.zeros((SUB, TILE), jnp.float32)
    start = tuple(tuple(row(chain, j) for j in range(4)) + (zero,) for chain in chains)
    lax.fori_loop(0, STEPS // UNROLL, forward, start)

    def value(n, k):
        return swept[n, pl.ds(pl.multiple_of(k * SUB, SUB), SUB)]

    carry = [zero] * count
    for k in range(WARM - 1, -1, -1):
        carry = [RATIO * carry[n] + value(n, k + WARM) for n in range(count)]
    sub = lax.broadcasted_iota(jnp.int32, (SUB, TILE), 0)
    beyond = RATIO / (1.0 - RATIO * RATIO)
    carry = [
        jnp.where(sub == SUB - 1, beyond * value(n, WARM + CHUNK - 1), pltpu.roll(carry[n], SUB - 1, 0))
        for n in range(count)
    ]

    def back(carry, k):
        carry = [RATIO * carry[n] + value(n, k + WARM) for n in range(count)]
        for n, (f, c) in enumerate(chains):
            at = pl.ds(k, SUB, stride=CHUNK)
            out[f, c, at] = carry[n] + z_part[f, c, at] if f < EARLY else carry[n]
        return carry

    def backward(step, carry):
        for u in range(UNROLL):
            carry = back(carry, CHUNK - 2 - (step * UNROLL + u))
        return tuple(carry)

    lax.fori_loop(0, CHUNK // UNROLL, backward, tuple(back(carry, CHUNK - 1)))
    matrix = difference_matrix()
    for f in range(EARLY, MIDDLE):
        for b in range(0, ROWS, 256):
            total = spanwise(field_rows(pad, f, b, 256), matrix)
            out[f, 0, pl.ds(b, 256)] += total[:, :TILE]
            out[f, 1, pl.ds(b, 256)] += total[:, TILE:]


def waits_longest():
    return lax.axis_index("gz") == 0


def first_kernel(pad, z_part, far_z_in, far_x, near_x, out, far_z, swept):
    pl.when(waits_longest())(lambda: inner_body(pad, z_part, out, swept))


def inner_kernel(pad, z_part, done, out, swept):
    pl.when(jnp.logical_not(waits_longest()))(lambda: inner_body(pad, z_part, out, swept))


def halo_columns(left, right, turned_in, turned_out):
    turned_in[0:EDGE] = left
    turned_in[EDGE:] = right
    l3, l2, l1 = (turned_in[n * GAP : n * GAP + TILE_ROWS] for n in range(3))
    r1, r2, r3 = (turned_in[EDGE + n * GAP : EDGE + n * GAP + TILE_ROWS] for n in range(3))
    none = jnp.zeros((TILE_ROWS, TILE), jnp.float32)
    for n, value in enumerate(
        (
            -0.75 * l1 + 0.15 * l2 - l3 * (1.0 / 60.0),
            0.15 * l1 - l2 * (1.0 / 60.0),
            l1 * (-1.0 / 60.0),
            none,
            none,
            r1 * (1.0 / 60.0),
            -0.15 * r1 + r2 * (1.0 / 60.0),
            0.75 * r1 - 0.15 * r2 + r3 * (1.0 / 60.0),
        )
    ):
        turned_out[n * GAP : n * GAP + TILE_ROWS] = value


def finish(sides, inner, before, after, out_hbm, work, turned_out, sems):
    copies = []
    place = lax.broadcasted_iota(jnp.int32, (HALO, TILE), 0)
    top, bottom = TAIL * powers(place), TAIL * powers(HALO - 1 - place)
    top_next, bottom_next = jnp.where(place == 0, NEXT, 0.0), jnp.where(place == HALO - 1, NEXT, 0.0)
    zeros = jnp.zeros((TILE - 2 * SUB, TILE), jnp.float32)
    lane = lax.broadcasted_iota(jnp.int32, (TILE, TILE), 1)
    half = ROWS // 2
    for f in range(FIELDS):
        for h in range(2):
            for b in range(h * BLOCKS // 2, (h + 1) * BLOCKS // 2):
                rows = pl.ds(b * TILE, TILE)
                columns = turned_out[pl.ds(f * BLOCKS + b, SUB, stride=GAP)]
                turned = jnp.concatenate([columns, zeros, columns]).T
                if 0 in sides:
                    work[f, 0, rows] = inner[f, 0, rows] + jnp.where(lane < 4, turned, 0.0)
                if 1 in sides:
                    work[f, 1, rows] = inner[f, 1, rows] + jnp.where(lane < TILE - 4, 0.0, turned)
            for c in sides:
                lanes = slice(c * TILE, (c + 1) * TILE)
                if h == 0:
                    work[f, c, pl.ds(0, HALO)] += (
                        top * before[2 * f : 2 * f + 1, lanes] + top_next * before[2 * f + 1 : 2 * f + 2, lanes]
                    )
                else:
                    work[f, c, pl.ds(ROWS - HALO, HALO)] -= (
                        bottom * after[2 * f : 2 * f + 1, lanes] + bottom_next * after[2 * f + 1 : 2 * f + 2, lanes]
                    )
                rows = pl.ds(h * half, half)
                copy = pltpu.make_async_copy(
                    work.at[f, c, rows], out_hbm.at[f, rows, pl.ds(c * TILE, TILE)], sems.at[f, c, h]
                )
                copy.start()
                copies.append(copy)
    for copy in copies:
        copy.wait()


def half_kernel(inner, near_z, far_x, near_x, out_hbm, work, turned_in, turned_out, sems):
    def body():
        even_x = is_even("gx")
        before = jnp.where(even_x, far_x[...], near_x[...])
        after = jnp.where(even_x, near_x[...], far_x[...])
        halo_columns(jnp.zeros((EDGE, TILE), jnp.float32), near_z[...], turned_in, turned_out)
        finish((1,), inner, before, after, out_hbm, work, turned_out, sems)

    pl.when(waits_longest())(body)


def edge_kernel(inner, far_z, near_z, far_x, near_x, half, out_hbm, work, turned_in, turned_out, sems):
    even_x, even_z = is_even("gx"), is_even("gz")
    before = jnp.where(even_x, far_x[...], near_x[...])
    after = jnp.where(even_x, near_x[...], far_x[...])
    left, right = jnp.where(even_z, far_z[...], near_z[...]), jnp.where(even_z, near_z[...], far_z[...])
    halo_columns(left, right, turned_in, turned_out)

    @pl.when(waits_longest())
    def _():
        finish((0,), inner, before, after, out_hbm, work, turned_out, sems)

    @pl.when(jnp.logical_not(waits_longest()))
    def _():
        finish((0, 1), inner, before, after, out_hbm, work, turned_out, sems)


def vmem_spec():
    return pl.BlockSpec(memory_space=pltpu.VMEM)


def any_spec():
    return pl.BlockSpec(memory_space=pl.ANY)


def in_vmem(value):
    return pltpu.with_memory_space_constraint(value, pltpu.VMEM)


def call(kernel, outs, scratch, ins, name, aliases=None, out_specs=None):
    return pl.pallas_call(
        kernel,
        out_shape=outs,
        in_specs=[any_spec() if value.ndim == 3 else vmem_spec() for value in ins],
        out_specs=out_specs or (vmem_spec(),) * len(outs),
        scratch_shapes=scratch,
        input_output_aliases=aliases or {},
        compiler_params=pltpu.CompilerParams(vmem_limit_bytes=16 * MIB),
        name=name,
    )(*ins)


def on_device(velocity):
    f32 = jnp.float32
    block = pltpu.VMEM((FIELDS, 2, LONG, TILE), f32)
    x_edge, z_edge = pltpu.VMEM((2 * FIELDS, LANES), f32), pltpu.VMEM((EDGE, TILE), f32)
    turned = pltpu.VMEM((400, TILE), f32)
    sems = pltpu.SemaphoreType.DMA((FIELDS, 2))
    swept = [pltpu.VMEM((2 * FIELDS, STEPS * SUB, TILE), f32)]
    pad, z_part, near_x, far_x, near_z, far_z = call(
        pack_kernel,
        (
            pltpu.VMEM((FIELDS, 2, PAD, TILE), f32),
            pltpu.VMEM((EARLY, 2, LONG, TILE), f32),
            x_edge,
            x_edge,
            z_edge,
            z_edge,
        ),
        [turned, turned, sems],
        [pltpu.with_memory_space_constraint(velocity, pltpu.HBM)],
        "pack",
    )

    def swap(value, axis, first):
        size = lax.axis_size(axis)
        pairs = [(i % size, (i + 1) % size) for i in range(first, size, 2)]
        return lax.ppermute(value, axis, pairs + [(j, i) for i, j in pairs])

    pad, z_part = in_vmem(pad), in_vmem(z_part)
    near_z, far_x, near_x = swap(near_z, "gz", 0), swap(far_x, "gx", 1), swap(near_x, "gx", 0)
    partial, far_z = call(first_kernel, (block, z_edge), swept, [pad, z_part, in_vmem(far_z), far_x, near_x], "first", {2: 1})
    far_z = swap(far_z, "gz", 1)
    (partial,) = call(inner_kernel, (block,), swept, [pad, z_part, in_vmem(partial)], "inner", {2: 0})
    partial = in_vmem(partial)
    work = [
        pltpu.VMEM((FIELDS, 2, ROWS, TILE), f32),
        pltpu.VMEM((2 * EDGE, TILE), f32),
        turned,
        pltpu.SemaphoreType.DMA((FIELDS, 2, 2)),
    ]
    whole = pltpu.HBM((FIELDS, ROWS, LANES), f32)
    half = call(half_kernel, whole, work, [partial, near_z, far_x, near_x], "half", None, any_spec())
    return call(
        edge_kernel, whole, work, [partial, far_z, near_z, far_x, near_x, half], "edges", {5: 0}, any_spec()
    )


def solution(mesh):
    return jax.shard_map(
        on_device,
        mesh=mesh,
        in_specs=(P(None, "gx", "gz"),),
        out_specs=P(None, "gx", "gz"),
        check_vma=False,
    )
```

```python
import math

import jax
import jax.numpy as jnp
import numpy as np
from jax import lax
from jax.experimental import pallas as pl
from jax.experimental.pallas import tpu as pltpu
from jax.sharding import PartitionSpec as P

FIELDS, ROWS, LANES = 4, 1536, 256
HALO = 24
PAD = 1576
SUB = 8
CHUNK = ROWS // SUB + 1
WARM = HALO - 2
STEPS = 216
UNROLL = 8
EARLY = 1
MIDDLE = 2
LONG = SUB * CHUNK
TILE = 128
BLOCKS = ROWS // TILE
TILE_ROWS = FIELDS * BLOCKS
RATIO = (math.sqrt(5.0) - 3.0) / 2.0
KAPPA = -1.0 / (3.0 * RATIO)
NEAR = 7.0 / 9.0 / KAPPA
FAR = 1.0 / 36.0 / KAPPA
MIB = 1 << 20


GAP = TILE_ROWS + 1
EDGE = 152
FAR_EDGE = 160
SCALE = 1.0 / (KAPPA * (1.0 - RATIO * RATIO))
TAIL = SCALE * (7.0 / 9.0 * (RATIO - 1.0 / RATIO) + 1.0 / 36.0 * (RATIO**2 - RATIO**-2))
NEXT = -1.0 / 12.0


def powers(exponent):
    value = jnp.where(exponent % 2 == 1, RATIO, 1.0)
    for bit in (2, 4, 8, 16):
        value = value * jnp.where((exponent // bit) % 2 == 1, RATIO**bit, 1.0)
    return value


def difference_matrix():
    gap = lax.broadcasted_iota(jnp.int32, (LANES, LANES), 0) - lax.broadcasted_iota(
        jnp.int32, (LANES, LANES), 1
    )
    size = jnp.abs(gap)
    weight = jnp.where(size == 1, 45.0, jnp.where(size == 2, -9.0, jnp.where(size == 3, 1.0, 0.0)))
    return jnp.where(gap < 0, -weight, weight).astype(jnp.bfloat16)


def spanwise(here, matrix):
    high = here.astype(jnp.bfloat16)
    rest = here - high.astype(jnp.float32)
    middle = rest.astype(jnp.bfloat16)
    low = (rest - middle.astype(jnp.float32)).astype(jnp.bfloat16)
    total = jnp.dot(high, matrix, preferred_element_type=jnp.float32)
    total += jnp.dot(middle, matrix, preferred_element_type=jnp.float32)
    total += jnp.dot(low, matrix, preferred_element_type=jnp.float32)
    return total * (1.0 / 60.0)


def field_rows(pad, f, row, count):
    rows = pl.ds(HALO + row, count)
    return jnp.concatenate([pad[f, 0, rows], pad[f, 1, rows]], axis=1)


def is_even(axis):
    return lax.rem(lax.axis_index(axis), 2) == 0


def pack_kernel(v_hbm, pad, z_part, near_x, far_x, near_z, far_z, turned_first, turned_last, sems):
    copies = []
    for f in range(FIELDS):
        for c in range(2):
            lanes = pl.ds(c * TILE, TILE)
            copy = pltpu.make_async_copy(v_hbm.at[f, :, lanes], pad.at[f, c, pl.ds(HALO, ROWS)], sems.at[f, c])
            copy.start()
            copies.append(copy)
    even_x, even_z = is_even("gx"), is_even("gz")
    matrix = difference_matrix()
    zeros = jnp.zeros((HALO, TILE), jnp.float32)
    for f in range(FIELDS):
        for c in range(2):
            pad[f, c, pl.ds(0, HALO)] = zeros
            pad[f, c, pl.ds(HALO + ROWS, PAD - HALO - ROWS)] = jnp.zeros((PAD - HALO - ROWS, TILE), jnp.float32)
    lane = lax.broadcasted_iota(jnp.int32, (TILE, TILE), 1)
    place = lax.broadcasted_iota(jnp.int32, (HALO, TILE), 0)
    head_weight, tail_weight = powers(place + 1), powers(HALO - place)
    for f in range(FIELDS):
        for c in range(2):
            copies[2 * f + c].wait()
        for c in range(2):
            lanes = pl.ds(c * TILE, TILE)
            head, tail = pad[f, c, pl.ds(HALO, HALO)], pad[f, c, pl.ds(ROWS, HALO)]
            head_sum = jnp.sum(head * head_weight, axis=0, keepdims=True)
            tail_sum = jnp.sum(tail * tail_weight, axis=0, keepdims=True)
            near_x[pl.ds(2 * f, 1), lanes] = jnp.where(even_x, tail_sum, head_sum)
            far_x[pl.ds(2 * f, 1), lanes] = jnp.where(even_x, head_sum, tail_sum)
            near_x[pl.ds(2 * f + 1, 1), lanes] = jnp.where(even_x, tail[HALO - 1 :], head[:1])
            far_x[pl.ds(2 * f + 1, 1), lanes] = jnp.where(even_x, head[:1], tail[HALO - 1 :])
        for b in range(BLOCKS):
            rows = pl.ds(HALO + b * TILE, TILE)
            turned = jnp.where(lane < 64, pad[f, 0, rows], pad[f, 1, rows]).T
            block = f * BLOCKS + b
            turned_first[pl.ds(block, SUB, stride=GAP)] = turned[:SUB]
            turned_last[pl.ds(block + 3, SUB, stride=GAP)] = turned[TILE - SUB :]
        if f < EARLY:
            for b in range(0, ROWS, 256):
                total = spanwise(field_rows(pad, f, b, 256), matrix)
                z_part[f, 0, pl.ds(b, 256)] = total[:, :TILE]
                z_part[f, 1, pl.ds(b, 256)] = total[:, TILE:]
    first, last = turned_first[0:EDGE], turned_last[5 * GAP + 3 : 5 * GAP + 3 + EDGE]
    near_z[...] = jnp.where(even_z, last, first)
    far_z[0:EDGE] = jnp.where(even_z, first, last)
    far_z[EDGE:] = jnp.zeros((FAR_EDGE - EDGE, TILE), jnp.float32)


def inner_body(pad, z_part, out, swept):
    chains = [(f, c) for f in range(FIELDS) for c in (0, 1)]
    count = len(chains)

    def row(chain, k):
        f, c = chain
        return pad[f, c, pl.ds(k, SUB, stride=CHUNK)]

    def forward(step, carry):
        carry = list(carry)
        for u in range(UNROLL):
            k = step * UNROLL + u
            for n, chain in enumerate(chains):
                back2, back1, here, ahead1, y = carry[n]
                ahead2 = row(chain, k + 4)
                y = RATIO * y + (NEAR * (ahead1 - back1) + FAR * (ahead2 - back2))
                swept[n, pl.ds(pl.multiple_of(k * SUB, SUB), SUB)] = y
                carry[n] = (back1, here, ahead1, ahead2, y)
        return tuple(carry)

    zero = jnp.zeros((SUB, TILE), jnp.float32)
    start = tuple(tuple(row(chain, j) for j in range(4)) + (zero,) for chain in chains)
    lax.fori_loop(0, STEPS // UNROLL, forward, start)

    def value(n, k):
        return swept[n, pl.ds(pl.multiple_of(k * SUB, SUB), SUB)]

    carry = [zero] * count
    for k in range(WARM - 1, -1, -1):
        carry = [RATIO * carry[n] + value(n, k + WARM) for n in range(count)]
    sub = lax.broadcasted_iota(jnp.int32, (SUB, TILE), 0)
    beyond = RATIO / (1.0 - RATIO * RATIO)
    carry = [
        jnp.where(sub == SUB - 1, beyond * value(n, WARM + CHUNK - 1), pltpu.roll(carry[n], SUB - 1, 0))
        for n in range(count)
    ]

    def back(carry, k):
        carry = [RATIO * carry[n] + value(n, k + WARM) for n in range(count)]
        for n, (f, c) in enumerate(chains):
            at = pl.ds(k, SUB, stride=CHUNK)
            out[f, c, at] = carry[n] + z_part[f, c, at] if f < EARLY else carry[n]
        return carry

    def backward(step, carry):
        for u in range(UNROLL):
            carry = back(carry, CHUNK - 2 - (step * UNROLL + u))
        return tuple(carry)

    lax.fori_loop(0, CHUNK // UNROLL, backward, tuple(back(carry, CHUNK - 1)))
    matrix = difference_matrix()
    for f in range(EARLY, MIDDLE):
        for b in range(0, ROWS, 256):
            total = spanwise(field_rows(pad, f, b, 256), matrix)
            out[f, 0, pl.ds(b, 256)] += total[:, :TILE]
            out[f, 1, pl.ds(b, 256)] += total[:, TILE:]


def place_z():
    return lax.axis_index("gz")


def first_kernel(pad, z_part, far_z_in, out, far_z, swept):
    pl.when(place_z() == 0)(lambda: inner_body(pad, z_part, out, swept))


def second_kernel(pad, z_part, done, near_z_in, near_x_in, far_x_in, out, near_z, near_x, far_x, swept):
    pl.when(place_z() == 1)(lambda: inner_body(pad, z_part, out, swept))


def inner_kernel(pad, z_part, done, out, swept):
    pl.when(place_z() > 1)(lambda: inner_body(pad, z_part, out, swept))


def edge_kernel(pad, inner, far_z, near_z, far_x, near_x, out_hbm, work, turned_in, turned_out, sems):
    copies = []
    even_x, even_z = is_even("gx"), is_even("gz")
    matrix = difference_matrix()
    near, far = near_z[...], far_z[0:EDGE]
    turned_in[0:EDGE] = jnp.where(even_z, far, near)
    turned_in[EDGE:] = jnp.where(even_z, near, far)
    l3, l2, l1 = (turned_in[n * GAP : n * GAP + TILE_ROWS] for n in range(3))
    r1, r2, r3 = (turned_in[EDGE + n * GAP : EDGE + n * GAP + TILE_ROWS] for n in range(3))
    none = jnp.zeros((TILE_ROWS, TILE), jnp.float32)
    for n, value in enumerate(
        (
            -0.75 * l1 + 0.15 * l2 - l3 * (1.0 / 60.0),
            0.15 * l1 - l2 * (1.0 / 60.0),
            l1 * (-1.0 / 60.0),
            none,
            none,
            r1 * (1.0 / 60.0),
            -0.15 * r1 + r2 * (1.0 / 60.0),
            0.75 * r1 - 0.15 * r2 + r3 * (1.0 / 60.0),
        )
    ):
        turned_out[n * GAP : n * GAP + TILE_ROWS] = value
    before, after = jnp.where(even_x, far_x[...], near_x[...]), jnp.where(even_x, near_x[...], far_x[...])
    place = lax.broadcasted_iota(jnp.int32, (HALO, TILE), 0)
    top, bottom = TAIL * powers(place), TAIL * powers(HALO - 1 - place)
    top_next, bottom_next = jnp.where(place == 0, NEXT, 0.0), jnp.where(place == HALO - 1, NEXT, 0.0)
    zeros = jnp.zeros((TILE - 2 * SUB, TILE), jnp.float32)
    lane = lax.broadcasted_iota(jnp.int32, (TILE, TILE), 1)
    for f in range(FIELDS):
        for b in range(BLOCKS):
            rows = pl.ds(b * TILE, TILE)
            columns = turned_out[pl.ds(f * BLOCKS + b, SUB, stride=GAP)]
            turned = jnp.concatenate([columns, zeros, columns]).T
            parts = [inner[f, c, rows] for c in range(2)]
            if f >= MIDDLE:
                total = spanwise(field_rows(pad, f, b * TILE, TILE), matrix)
                parts = [parts[c] + total[:, c * TILE : (c + 1) * TILE] for c in range(2)]
            work[f, 0, rows] = parts[0] + jnp.where(lane < 4, turned, 0.0)
            work[f, 1, rows] = parts[1] + jnp.where(lane < TILE - 4, 0.0, turned)
        for c in range(2):
            lanes = slice(c * TILE, (c + 1) * TILE)
            work[f, c, pl.ds(0, HALO)] += (
                top * before[2 * f : 2 * f + 1, lanes] + top_next * before[2 * f + 1 : 2 * f + 2, lanes]
            )
            work[f, c, pl.ds(ROWS - HALO, HALO)] -= (
                bottom * after[2 * f : 2 * f + 1, lanes] + bottom_next * after[2 * f + 1 : 2 * f + 2, lanes]
            )
            copy = pltpu.make_async_copy(work.at[f, c], out_hbm.at[f, :, pl.ds(c * TILE, TILE)], sems.at[f, c])
            copy.start()
            copies.append(copy)
    for copy in copies:
        copy.wait()


def vmem_spec():
    return pl.BlockSpec(memory_space=pltpu.VMEM)


def any_spec():
    return pl.BlockSpec(memory_space=pl.ANY)


def in_vmem(value):
    return pltpu.with_memory_space_constraint(value, pltpu.VMEM)


def call(kernel, outs, scratch, ins, name, aliases=None, out_specs=None):
    return pl.pallas_call(
        kernel,
        out_shape=outs,
        in_specs=[any_spec() if name == "pack" else vmem_spec() for _ in ins],
        out_specs=out_specs or (vmem_spec(),) * len(outs),
        scratch_shapes=scratch,
        input_output_aliases=aliases or {},
        compiler_params=pltpu.CompilerParams(vmem_limit_bytes=16 * MIB),
        name=name,
    )(*ins)


def on_device(velocity):
    f32 = jnp.float32
    block = pltpu.VMEM((FIELDS, 2, LONG, TILE), f32)
    x_edge, z_edge = pltpu.VMEM((2 * FIELDS, LANES), f32), pltpu.VMEM((EDGE, TILE), f32)
    far_edge = pltpu.VMEM((FAR_EDGE, TILE), f32)
    turned = pltpu.VMEM((400, TILE), f32)
    sems = pltpu.SemaphoreType.DMA((FIELDS, 2))
    swept = [pltpu.VMEM((2 * FIELDS, STEPS * SUB, TILE), f32)]
    pad, z_part, near_x, far_x, near_z, far_z = call(
        pack_kernel,
        (
            pltpu.VMEM((FIELDS, 2, PAD, TILE), f32),
            pltpu.VMEM((EARLY, 2, LONG, TILE), f32),
            x_edge,
            x_edge,
            z_edge,
            far_edge,
        ),
        [turned, turned, sems],
        [pltpu.with_memory_space_constraint(velocity, pltpu.HBM)],
        "pack",
    )

    def swap(value, axis, first):
        size = lax.axis_size(axis)
        pairs = [(i % size, (i + 1) % size) for i in range(first, size, 2)]
        return lax.ppermute(value, axis, pairs + [(j, i) for i, j in pairs])

    pad, z_part = in_vmem(pad), in_vmem(z_part)
    partial, far_z = call(first_kernel, (block, far_edge), swept, [pad, z_part, in_vmem(far_z)], "first", {2: 1})
    far_z = swap(far_z, "gz", 1)
    partial, near_z, near_x, far_x = call(
        second_kernel,
        (block, z_edge, x_edge, x_edge),
        swept,
        [pad, z_part, in_vmem(partial), in_vmem(near_z), in_vmem(near_x), in_vmem(far_x)],
        "second",
        {2: 0, 3: 1, 4: 2, 5: 3},
    )
    near_z = swap(near_z, "gz", 0)
    near_x, far_x = swap(near_x, "gx", 0), swap(far_x, "gx", 1)
    (partial,) = call(inner_kernel, (block,), swept, [pad, z_part, in_vmem(partial)], "inner", {2: 0})
    return call(
        edge_kernel,
        jax.ShapeDtypeStruct((FIELDS, ROWS, LANES), f32),
        [pltpu.VMEM((FIELDS, 2, ROWS, TILE), f32), pltpu.VMEM((2 * EDGE, TILE), f32), turned, sems],
        [pad, in_vmem(partial), far_z, near_z, far_x, near_x],
        "edges",
        None,
        any_spec(),
    )


def solution(mesh):
    return jax.shard_map(
        on_device,
        mesh=mesh,
        in_specs=(P(None, "gx", "gz"),),
        out_specs=P(None, "gx", "gz"),
        check_vma=False,
    )
```

```python
import math

import jax
import jax.numpy as jnp
import numpy as np
from jax import lax
from jax.experimental import pallas as pl
from jax.experimental.pallas import tpu as pltpu
from jax.sharding import PartitionSpec as P

FIELDS, ROWS, LANES = 4, 1536, 256
HALO = 24
PAD = 1576
SUB = 8
CHUNK = ROWS // SUB + 1
WARM = HALO - 2
STEPS = 216
UNROLL = 8
EARLY = 1
MIDDLE = 2
LONG = SUB * CHUNK
TILE = 128
BLOCKS = ROWS // TILE
TILE_ROWS = FIELDS * BLOCKS
RATIO = (math.sqrt(5.0) - 3.0) / 2.0
KAPPA = -1.0 / (3.0 * RATIO)
NEAR = 7.0 / 9.0 / KAPPA
FAR = 1.0 / 36.0 / KAPPA
MIB = 1 << 20


GAP = TILE_ROWS + 1
EDGE = 152
FAR_EDGE = 160
SCALE = 1.0 / (KAPPA * (1.0 - RATIO * RATIO))
TAIL = SCALE * (7.0 / 9.0 * (RATIO - 1.0 / RATIO) + 1.0 / 36.0 * (RATIO**2 - RATIO**-2))
NEXT = -1.0 / 12.0


def powers(exponent):
    value = jnp.where(exponent % 2 == 1, RATIO, 1.0)
    for bit in (2, 4, 8, 16):
        value = value * jnp.where((exponent // bit) % 2 == 1, RATIO**bit, 1.0)
    return value


def difference_matrix():
    gap = lax.broadcasted_iota(jnp.int32, (LANES, LANES), 0) - lax.broadcasted_iota(
        jnp.int32, (LANES, LANES), 1
    )
    size = jnp.abs(gap)
    weight = jnp.where(size == 1, 45.0, jnp.where(size == 2, -9.0, jnp.where(size == 3, 1.0, 0.0)))
    return jnp.where(gap < 0, -weight, weight).astype(jnp.bfloat16)


def spanwise(here, matrix):
    high = here.astype(jnp.bfloat16)
    rest = here - high.astype(jnp.float32)
    middle = rest.astype(jnp.bfloat16)
    low = (rest - middle.astype(jnp.float32)).astype(jnp.bfloat16)
    total = jnp.dot(high, matrix, preferred_element_type=jnp.float32)
    total += jnp.dot(middle, matrix, preferred_element_type=jnp.float32)
    total += jnp.dot(low, matrix, preferred_element_type=jnp.float32)
    return total * (1.0 / 60.0)


def field_rows(pad, f, row, count):
    rows = pl.ds(HALO + row, count)
    return jnp.concatenate([pad[f, 0, rows], pad[f, 1, rows]], axis=1)


def is_even(axis):
    return lax.rem(lax.axis_index(axis), 2) == 0


def pack_kernel(v_hbm, pad, z_part, near_x, far_x, near_z, far_z, turned_first, turned_last, sems):
    copies = []
    for f in range(FIELDS):
        for c in range(2):
            lanes = pl.ds(c * TILE, TILE)
            copy = pltpu.make_async_copy(v_hbm.at[f, :, lanes], pad.at[f, c, pl.ds(HALO, ROWS)], sems.at[f, c])
            copy.start()
            copies.append(copy)
    even_x, even_z = is_even("gx"), is_even("gz")
    matrix = difference_matrix()
    zeros = jnp.zeros((HALO, TILE), jnp.float32)
    for f in range(FIELDS):
        for c in range(2):
            pad[f, c, pl.ds(0, HALO)] = zeros
            pad[f, c, pl.ds(HALO + ROWS, PAD - HALO - ROWS)] = jnp.zeros((PAD - HALO - ROWS, TILE), jnp.float32)
    lane = lax.broadcasted_iota(jnp.int32, (TILE, TILE), 1)
    place = lax.broadcasted_iota(jnp.int32, (HALO, TILE), 0)
    head_weight, tail_weight = powers(place + 1), powers(HALO - place)
    for f in range(FIELDS):
        for c in range(2):
            copies[2 * f + c].wait()
        for c in range(2):
            lanes = pl.ds(c * TILE, TILE)
            head, tail = pad[f, c, pl.ds(HALO, HALO)], pad[f, c, pl.ds(ROWS, HALO)]
            head_sum = jnp.sum(head * head_weight, axis=0, keepdims=True)
            tail_sum = jnp.sum(tail * tail_weight, axis=0, keepdims=True)
            near_x[pl.ds(2 * f, 1), lanes] = jnp.where(even_x, tail_sum, head_sum)
            far_x[pl.ds(2 * f, 1), lanes] = jnp.where(even_x, head_sum, tail_sum)
            near_x[pl.ds(2 * f + 1, 1), lanes] = jnp.where(even_x, tail[HALO - 1 :], head[:1])
            far_x[pl.ds(2 * f + 1, 1), lanes] = jnp.where(even_x, head[:1], tail[HALO - 1 :])
        for b in range(BLOCKS):
            rows = pl.ds(HALO + b * TILE, TILE)
            turned = jnp.where(lane < 64, pad[f, 0, rows], pad[f, 1, rows]).T
            block = f * BLOCKS + b
            turned_first[pl.ds(block, SUB, stride=GAP)] = turned[:SUB]
            turned_last[pl.ds(block + 3, SUB, stride=GAP)] = turned[TILE - SUB :]
        if f < EARLY:
            for b in range(0, ROWS, 256):
                total = spanwise(field_rows(pad, f, b, 256), matrix)
                z_part[f, 0, pl.ds(b, 256)] = total[:, :TILE]
                z_part[f, 1, pl.ds(b, 256)] = total[:, TILE:]
    first, last = turned_first[0:EDGE], turned_last[5 * GAP + 3 : 5 * GAP + 3 + EDGE]
    near_z[...] = jnp.where(even_z, last, first)
    far_z[0:EDGE] = jnp.where(even_z, first, last)
    far_z[EDGE:] = jnp.zeros((FAR_EDGE - EDGE, TILE), jnp.float32)


def inner_body(pad, z_part, out, swept):
    chains = [(f, c) for f in range(FIELDS) for c in (0, 1)]
    count = len(chains)

    def row(chain, k):
        f, c = chain
        return pad[f, c, pl.ds(k, SUB, stride=CHUNK)]

    def forward(step, carry):
        carry = list(carry)
        for u in range(UNROLL):
            k = step * UNROLL + u
            for n, chain in enumerate(chains):
                back2, back1, here, ahead1, y = carry[n]
                ahead2 = row(chain, k + 4)
                y = RATIO * y + (NEAR * (ahead1 - back1) + FAR * (ahead2 - back2))
                swept[n, pl.ds(pl.multiple_of(k * SUB, SUB), SUB)] = y
                carry[n] = (back1, here, ahead1, ahead2, y)
        return tuple(carry)

    zero = jnp.zeros((SUB, TILE), jnp.float32)
    start = tuple(tuple(row(chain, j) for j in range(4)) + (zero,) for chain in chains)
    lax.fori_loop(0, STEPS // UNROLL, forward, start)

    def value(n, k):
        return swept[n, pl.ds(pl.multiple_of(k * SUB, SUB), SUB)]

    carry = [zero] * count
    for k in range(WARM - 1, -1, -1):
        carry = [RATIO * carry[n] + value(n, k + WARM) for n in range(count)]
    sub = lax.broadcasted_iota(jnp.int32, (SUB, TILE), 0)
    beyond = RATIO / (1.0 - RATIO * RATIO)
    carry = [
        jnp.where(sub == SUB - 1, beyond * value(n, WARM + CHUNK - 1), pltpu.roll(carry[n], SUB - 1, 0))
        for n in range(count)
    ]

    def back(carry, k):
        carry = [RATIO * carry[n] + value(n, k + WARM) for n in range(count)]
        for n, (f, c) in enumerate(chains):
            at = pl.ds(k, SUB, stride=CHUNK)
            out[f, c, at] = carry[n] + z_part[f, c, at] if f < EARLY else carry[n]
        return carry

    def backward(step, carry):
        for u in range(UNROLL):
            carry = back(carry, CHUNK - 2 - (step * UNROLL + u))
        return tuple(carry)

    lax.fori_loop(0, CHUNK // UNROLL, backward, tuple(back(carry, CHUNK - 1)))
    add_spanwise(pad, out, range(EARLY, MIDDLE))


def add_spanwise(pad, out, fields):
    matrix = difference_matrix()
    for f in fields:
        for b in range(0, ROWS, 256):
            total = spanwise(field_rows(pad, f, b, 256), matrix)
            out[f, 0, pl.ds(b, 256)] += total[:, :TILE]
            out[f, 1, pl.ds(b, 256)] += total[:, TILE:]


def place_z():
    return lax.axis_index("gz")


def first_kernel(pad, z_part, far_z_in, out, far_z, swept):
    pl.when(place_z() == 0)(lambda: inner_body(pad, z_part, out, swept))


def second_kernel(pad, z_part, done, near_z_in, near_x_in, far_x_in, out, near_z, near_x, far_x, swept):
    @pl.when(place_z() == 1)
    def _():
        inner_body(pad, z_part, out, swept)
        add_spanwise(pad, out, range(MIDDLE, FIELDS))


def inner_kernel(pad, z_part, done, out, swept):
    pl.when(place_z() > 1)(lambda: inner_body(pad, z_part, out, swept))
    pl.when(place_z() == 0)(lambda: add_spanwise(pad, out, range(MIDDLE, FIELDS)))


def halo_columns(left, right, turned_in, turned_out):
    turned_in[0:EDGE] = left
    turned_in[EDGE:] = right
    l3, l2, l1 = (turned_in[n * GAP : n * GAP + TILE_ROWS] for n in range(3))
    r1, r2, r3 = (turned_in[EDGE + n * GAP : EDGE + n * GAP + TILE_ROWS] for n in range(3))
    none = jnp.zeros((TILE_ROWS, TILE), jnp.float32)
    for n, value in enumerate(
        (
            -0.75 * l1 + 0.15 * l2 - l3 * (1.0 / 60.0),
            0.15 * l1 - l2 * (1.0 / 60.0),
            l1 * (-1.0 / 60.0),
            none,
            none,
            r1 * (1.0 / 60.0),
            -0.15 * r1 + r2 * (1.0 / 60.0),
            0.75 * r1 - 0.15 * r2 + r3 * (1.0 / 60.0),
        )
    ):
        turned_out[n * GAP : n * GAP + TILE_ROWS] = value


def finish(whole, rims, middles, late, pad, inner, before, after, out_hbm, work, turned_out, sems):
    copies = []
    matrix = difference_matrix()
    place = lax.broadcasted_iota(jnp.int32, (HALO, TILE), 0)
    top, bottom = TAIL * powers(place), TAIL * powers(HALO - 1 - place)
    top_next, bottom_next = jnp.where(place == 0, NEXT, 0.0), jnp.where(place == HALO - 1, NEXT, 0.0)
    zeros = jnp.zeros((TILE - 2 * SUB, TILE), jnp.float32)
    lane = lax.broadcasted_iota(jnp.int32, (TILE, TILE), 1)
    own = (lane < 4, lane >= TILE - 4)
    half = ROWS // 2
    for f in range(FIELDS):
        for h in range(2):
            for b in range(h * BLOCKS // 2, (h + 1) * BLOCKS // 2):
                rows = pl.ds(b * TILE, TILE)
                columns = turned_out[pl.ds(f * BLOCKS + b, SUB, stride=GAP)]
                turned = jnp.concatenate([columns, zeros, columns]).T
                if late and f >= MIDDLE:
                    total = spanwise(field_rows(pad, f, b * TILE, TILE), matrix)
                for c in whole + middles + (rims if b in (0, BLOCKS - 1) else ()):
                    value = inner[f, c, rows]
                    if late and f >= MIDDLE:
                        value = value + total[:, c * TILE : (c + 1) * TILE]
                    work[f, c, rows] = value + jnp.where(own[c], turned, 0.0)
            outer = pl.ds(0, HALO) if h == 0 else pl.ds(ROWS - HALO, HALO)
            for c in whole + rims:
                lanes = slice(c * TILE, (c + 1) * TILE)
                if h == 0:
                    work[f, c, outer] += (
                        top * before[2 * f : 2 * f + 1, lanes] + top_next * before[2 * f + 1 : 2 * f + 2, lanes]
                    )
                else:
                    work[f, c, outer] -= (
                        bottom * after[2 * f : 2 * f + 1, lanes] + bottom_next * after[2 * f + 1 : 2 * f + 2, lanes]
                    )
            for c in whole + rims + middles:
                rows = outer
                if c in whole:
                    rows = pl.ds(h * half, half)
                elif c in middles:
                    rows = pl.ds(HALO if h == 0 else half, half - HALO)
                copy = pltpu.make_async_copy(
                    work.at[f, c, rows], out_hbm.at[f, rows, pl.ds(c * TILE, TILE)], sems.at[f, c, h]
                )
                copy.start()
                copies.append(copy)
    for copy in copies:
        copy.wait()


def half_kernel(pad, inner, far_z, out_hbm, work, turned_in, turned_out, sems):
    @pl.when(place_z() == 1)
    def _():
        halo_columns(jnp.zeros((EDGE, TILE), jnp.float32), far_z[0:EDGE], turned_in, turned_out)
        finish((), (), (1,), False, pad, inner, None, None, out_hbm, work, turned_out, sems)


def edge_kernel(pad, inner, far_z, near_z, far_x, near_x, half, out_hbm, work, turned_in, turned_out, sems):
    even_x, even_z = is_even("gx"), is_even("gz")
    before = jnp.where(even_x, far_x[...], near_x[...])
    after = jnp.where(even_x, near_x[...], far_x[...])
    near, far = near_z[...], far_z[0:EDGE]
    halo_columns(jnp.where(even_z, far, near), jnp.where(even_z, near, far), turned_in, turned_out)
    rest = (pad, inner, before, after, out_hbm, work, turned_out, sems)
    pl.when(place_z() == 0)(lambda: finish((0, 1), (), (), False, *rest))
    pl.when(place_z() == 1)(lambda: finish((0,), (1,), (), False, *rest))
    pl.when(place_z() > 1)(lambda: finish((0, 1), (), (), True, *rest))


def vmem_spec():
    return pl.BlockSpec(memory_space=pltpu.VMEM)


def any_spec():
    return pl.BlockSpec(memory_space=pl.ANY)


def in_vmem(value):
    return pltpu.with_memory_space_constraint(value, pltpu.VMEM)


def call(kernel, outs, scratch, ins, name, aliases=None, out_specs=None):
    return pl.pallas_call(
        kernel,
        out_shape=outs,
        in_specs=[any_spec() if value.ndim == 3 else vmem_spec() for value in ins],
        out_specs=out_specs or (vmem_spec(),) * len(outs),
        scratch_shapes=scratch,
        input_output_aliases=aliases or {},
        compiler_params=pltpu.CompilerParams(vmem_limit_bytes=16 * MIB),
        name=name,
    )(*ins)


def on_device(velocity):
    f32 = jnp.float32
    block = pltpu.VMEM((FIELDS, 2, LONG, TILE), f32)
    x_edge, z_edge = pltpu.VMEM((2 * FIELDS, LANES), f32), pltpu.VMEM((EDGE, TILE), f32)
    far_edge = pltpu.VMEM((FAR_EDGE, TILE), f32)
    turned = pltpu.VMEM((400, TILE), f32)
    swept = [pltpu.VMEM((2 * FIELDS, STEPS * SUB, TILE), f32)]
    pad, z_part, near_x, far_x, near_z, far_z = call(
        pack_kernel,
        (
            pltpu.VMEM((FIELDS, 2, PAD, TILE), f32),
            pltpu.VMEM((EARLY, 2, LONG, TILE), f32),
            x_edge,
            x_edge,
            z_edge,
            far_edge,
        ),
        [turned, turned, pltpu.SemaphoreType.DMA((FIELDS, 2))],
        [pltpu.with_memory_space_constraint(velocity, pltpu.HBM)],
        "pack",
    )

    def swap(value, axis, first):
        size = lax.axis_size(axis)
        pairs = [(i % size, (i + 1) % size) for i in range(first, size, 2)]
        return lax.ppermute(value, axis, pairs + [(j, i) for i, j in pairs])

    pad, z_part = in_vmem(pad), in_vmem(z_part)
    partial, far_z = call(first_kernel, (block, far_edge), swept, [pad, z_part, in_vmem(far_z)], "first", {2: 1})
    far_z = swap(far_z, "gz", 1)
    partial, near_z, near_x, far_x = call(
        second_kernel,
        (block, z_edge, x_edge, x_edge),
        swept,
        [pad, z_part, in_vmem(partial), in_vmem(near_z), in_vmem(near_x), in_vmem(far_x)],
        "second",
        {2: 0, 3: 1, 4: 2, 5: 3},
    )
    near_z = swap(near_z, "gz", 0)
    near_x, far_x = swap(near_x, "gx", 0), swap(far_x, "gx", 1)
    (partial,) = call(inner_kernel, (block,), swept, [pad, z_part, in_vmem(partial)], "inner", {2: 0})
    partial = in_vmem(partial)
    work = [
        pltpu.VMEM((FIELDS, 2, ROWS, TILE), f32),
        pltpu.VMEM((2 * EDGE, TILE), f32),
        turned,
        pltpu.SemaphoreType.DMA((FIELDS, 2, 2)),
    ]
    whole = pltpu.HBM((FIELDS, ROWS, LANES), f32)
    half = call(half_kernel, whole, work, [pad, partial, far_z], "half", None, any_spec())
    return call(
        edge_kernel,
        whole,
        work,
        [pad, partial, far_z, near_z, far_x, near_x, half],
        "edges",
        {6: 0},
        any_spec(),
    )


def solution(mesh):
    return jax.shard_map(
        on_device,
        mesh=mesh,
        in_specs=(P(None, "gx", "gz"),),
        out_specs=P(None, "gx", "gz"),
        check_vma=False,
    )
```

```python
import math

import jax
import jax.numpy as jnp
import numpy as np
from jax import lax
from jax.experimental import pallas as pl
from jax.experimental.pallas import tpu as pltpu
from jax.sharding import PartitionSpec as P

FIELDS, ROWS, LANES = 4, 1536, 256
HALO = 24
PAD = 1576
SUB = 8
CHUNK = ROWS // SUB + 1
WARM = HALO - 2
STEPS = 216
UNROLL = 8
EARLY = 1
MIDDLE = 2
LONG = SUB * CHUNK
TILE = 128
BLOCKS = ROWS // TILE
TILE_ROWS = FIELDS * BLOCKS
RATIO = (math.sqrt(5.0) - 3.0) / 2.0
KAPPA = -1.0 / (3.0 * RATIO)
NEAR = 7.0 / 9.0 / KAPPA
FAR = 1.0 / 36.0 / KAPPA
MIB = 1 << 20


GAP = TILE_ROWS + 1
EDGE = 152
FAR_EDGE = 160
SCALE = 1.0 / (KAPPA * (1.0 - RATIO * RATIO))
TAIL = SCALE * (7.0 / 9.0 * (RATIO - 1.0 / RATIO) + 1.0 / 36.0 * (RATIO**2 - RATIO**-2))
NEXT = -1.0 / 12.0


def powers(exponent):
    value = jnp.where(exponent % 2 == 1, RATIO, 1.0)
    for bit in (2, 4, 8, 16):
        value = value * jnp.where((exponent // bit) % 2 == 1, RATIO**bit, 1.0)
    return value


def difference_matrix():
    gap = lax.broadcasted_iota(jnp.int32, (LANES, LANES), 0) - lax.broadcasted_iota(
        jnp.int32, (LANES, LANES), 1
    )
    size = jnp.abs(gap)
    weight = jnp.where(size == 1, 45.0, jnp.where(size == 2, -9.0, jnp.where(size == 3, 1.0, 0.0)))
    return jnp.where(gap < 0, -weight, weight).astype(jnp.bfloat16)


def spanwise(here, matrix):
    high = here.astype(jnp.bfloat16)
    rest = here - high.astype(jnp.float32)
    middle = rest.astype(jnp.bfloat16)
    low = (rest - middle.astype(jnp.float32)).astype(jnp.bfloat16)
    total = jnp.dot(high, matrix, preferred_element_type=jnp.float32)
    total += jnp.dot(middle, matrix, preferred_element_type=jnp.float32)
    total += jnp.dot(low, matrix, preferred_element_type=jnp.float32)
    return total * (1.0 / 60.0)


def field_rows(pad, f, row, count):
    rows = pl.ds(HALO + row, count)
    return jnp.concatenate([pad[f, 0, rows], pad[f, 1, rows]], axis=1)


def is_even(axis):
    return lax.rem(lax.axis_index(axis), 2) == 0


def pack_kernel(v_hbm, pad, z_part, near_x, far_x, near_z, far_z, turned_first, turned_last, sems):
    copies = []
    for f in range(FIELDS):
        for c in range(2):
            lanes = pl.ds(c * TILE, TILE)
            copy = pltpu.make_async_copy(v_hbm.at[f, :, lanes], pad.at[f, c, pl.ds(HALO, ROWS)], sems.at[f, c])
            copy.start()
            copies.append(copy)
    even_x, even_z = is_even("gx"), is_even("gz")
    matrix = difference_matrix()
    zeros = jnp.zeros((HALO, TILE), jnp.float32)
    for f in range(FIELDS):
        for c in range(2):
            pad[f, c, pl.ds(0, HALO)] = zeros
            pad[f, c, pl.ds(HALO + ROWS, PAD - HALO - ROWS)] = jnp.zeros((PAD - HALO - ROWS, TILE), jnp.float32)
    lane = lax.broadcasted_iota(jnp.int32, (TILE, TILE), 1)
    place = lax.broadcasted_iota(jnp.int32, (HALO, TILE), 0)
    head_weight, tail_weight = powers(place + 1), powers(HALO - place)
    for f in range(FIELDS):
        for c in range(2):
            copies[2 * f + c].wait()
        for c in range(2):
            lanes = pl.ds(c * TILE, TILE)
            head, tail = pad[f, c, pl.ds(HALO, HALO)], pad[f, c, pl.ds(ROWS, HALO)]
            head_sum = jnp.sum(head * head_weight, axis=0, keepdims=True)
            tail_sum = jnp.sum(tail * tail_weight, axis=0, keepdims=True)
            near_x[pl.ds(2 * f, 1), lanes] = jnp.where(even_x, tail_sum, head_sum)
            far_x[pl.ds(2 * f, 1), lanes] = jnp.where(even_x, head_sum, tail_sum)
            near_x[pl.ds(2 * f + 1, 1), lanes] = jnp.where(even_x, tail[HALO - 1 :], head[:1])
            far_x[pl.ds(2 * f + 1, 1), lanes] = jnp.where(even_x, head[:1], tail[HALO - 1 :])
        for b in range(BLOCKS):
            rows = pl.ds(HALO + b * TILE, TILE)
            turned = jnp.where(lane < 64, pad[f, 0, rows], pad[f, 1, rows]).T
            block = f * BLOCKS + b
            turned_first[pl.ds(block, SUB, stride=GAP)] = turned[:SUB]
            turned_last[pl.ds(block + 3, SUB, stride=GAP)] = turned[TILE - SUB :]
        if f < EARLY:
            for b in range(0, ROWS, 256):
                total = spanwise(field_rows(pad, f, b, 256), matrix)
                z_part[f, 0, pl.ds(b, 256)] = total[:, :TILE]
                z_part[f, 1, pl.ds(b, 256)] = total[:, TILE:]
    first, last = turned_first[0:EDGE], turned_last[5 * GAP + 3 : 5 * GAP + 3 + EDGE]
    near_z[...] = jnp.where(even_z, last, first)
    far_z[0:EDGE] = jnp.where(even_z, first, last)
    far_z[EDGE:] = jnp.zeros((FAR_EDGE - EDGE, TILE), jnp.float32)


def inner_body(pad, z_part, out, swept):
    chains = [(f, c) for f in range(FIELDS) for c in (0, 1)]
    count = len(chains)

    def row(chain, k):
        f, c = chain
        return pad[f, c, pl.ds(k, SUB, stride=CHUNK)]

    def forward(step, carry):
        carry = list(carry)
        for u in range(UNROLL):
            k = step * UNROLL + u
            for n, chain in enumerate(chains):
                back2, back1, here, ahead1, y = carry[n]
                ahead2 = row(chain, k + 4)
                y = RATIO * y + (NEAR * (ahead1 - back1) + FAR * (ahead2 - back2))
                swept[n, pl.ds(pl.multiple_of(k * SUB, SUB), SUB)] = y
                carry[n] = (back1, here, ahead1, ahead2, y)
        return tuple(carry)

    zero = jnp.zeros((SUB, TILE), jnp.float32)
    start = tuple(tuple(row(chain, j) for j in range(4)) + (zero,) for chain in chains)
    lax.fori_loop(0, STEPS // UNROLL, forward, start)

    def value(n, k):
        return swept[n, pl.ds(pl.multiple_of(k * SUB, SUB), SUB)]

    carry = [zero] * count
    for k in range(WARM - 1, -1, -1):
        carry = [RATIO * carry[n] + value(n, k + WARM) for n in range(count)]
    sub = lax.broadcasted_iota(jnp.int32, (SUB, TILE), 0)
    beyond = RATIO / (1.0 - RATIO * RATIO)
    carry = [
        jnp.where(sub == SUB - 1, beyond * value(n, WARM + CHUNK - 1), pltpu.roll(carry[n], SUB - 1, 0))
        for n in range(count)
    ]

    def back(carry, k):
        carry = [RATIO * carry[n] + value(n, k + WARM) for n in range(count)]
        for n, (f, c) in enumerate(chains):
            at = pl.ds(k, SUB, stride=CHUNK)
            out[f, c, at] = carry[n] + z_part[f, c, at] if f < EARLY else carry[n]
        return carry

    def backward(step, carry):
        for u in range(UNROLL):
            carry = back(carry, CHUNK - 2 - (step * UNROLL + u))
        return tuple(carry)

    lax.fori_loop(0, CHUNK // UNROLL, backward, tuple(back(carry, CHUNK - 1)))
    add_spanwise(pad, out, range(EARLY, MIDDLE))


def add_spanwise(pad, out, fields):
    matrix = difference_matrix()
    for f in fields:
        for b in range(0, ROWS, 256):
            total = spanwise(field_rows(pad, f, b, 256), matrix)
            out[f, 0, pl.ds(b, 256)] += total[:, :TILE]
            out[f, 1, pl.ds(b, 256)] += total[:, TILE:]


def place_z():
    return lax.axis_index("gz")


def first_kernel(pad, z_part, far_z_in, out, far_z, swept):
    pl.when(place_z() == 0)(lambda: inner_body(pad, z_part, out, swept))


def second_kernel(pad, z_part, done, near_z_in, near_x_in, far_x_in, out, near_z, near_x, far_x, swept):
    @pl.when(place_z() == 1)
    def _():
        inner_body(pad, z_part, out, swept)
        add_spanwise(pad, out, range(MIDDLE, FIELDS))


def inner_kernel(pad, z_part, done, out, swept):
    pl.when(place_z() > 1)(lambda: inner_body(pad, z_part, out, swept))
    pl.when(place_z() == 0)(lambda: add_spanwise(pad, out, range(MIDDLE, FIELDS)))


def halo_columns(left, right, turned_in, turned_out):
    turned_in[0:EDGE] = left
    turned_in[EDGE:] = right
    l3, l2, l1 = (turned_in[n * GAP : n * GAP + TILE_ROWS] for n in range(3))
    r1, r2, r3 = (turned_in[EDGE + n * GAP : EDGE + n * GAP + TILE_ROWS] for n in range(3))
    none = jnp.zeros((TILE_ROWS, TILE), jnp.float32)
    for n, value in enumerate(
        (
            -0.75 * l1 + 0.15 * l2 - l3 * (1.0 / 60.0),
            0.15 * l1 - l2 * (1.0 / 60.0),
            l1 * (-1.0 / 60.0),
            none,
            none,
            r1 * (1.0 / 60.0),
            -0.15 * r1 + r2 * (1.0 / 60.0),
            0.75 * r1 - 0.15 * r2 + r3 * (1.0 / 60.0),
        )
    ):
        turned_out[n * GAP : n * GAP + TILE_ROWS] = value


def finish(whole, rims, middles, late, pad, inner, before, after, out_hbm, work, turned_out, sems):
    copies = []
    matrix = difference_matrix()
    place = lax.broadcasted_iota(jnp.int32, (HALO, TILE), 0)
    top, bottom = TAIL * powers(place), TAIL * powers(HALO - 1 - place)
    top_next, bottom_next = jnp.where(place == 0, NEXT, 0.0), jnp.where(place == HALO - 1, NEXT, 0.0)
    zeros = jnp.zeros((TILE - 2 * SUB, TILE), jnp.float32)
    lane = lax.broadcasted_iota(jnp.int32, (TILE, TILE), 1)
    own = (lane < 4, lane >= TILE - 4)
    half = ROWS // 2
    for f in range(FIELDS):
        for h in range(2):
            for b in range(h * BLOCKS // 2, (h + 1) * BLOCKS // 2):
                rows = pl.ds(b * TILE, TILE)
                columns = turned_out[pl.ds(f * BLOCKS + b, SUB, stride=GAP)]
                turned = jnp.concatenate([columns, zeros, columns]).T
                if late and f >= MIDDLE:
                    total = spanwise(field_rows(pad, f, b * TILE, TILE), matrix)
                for c in whole + middles + (rims if b in (0, BLOCKS - 1) else ()):
                    value = inner[f, c, rows]
                    if late and f >= MIDDLE:
                        value = value + total[:, c * TILE : (c + 1) * TILE]
                    work[f, c, rows] = value + jnp.where(own[c], turned, 0.0)
            outer = pl.ds(0, HALO) if h == 0 else pl.ds(ROWS - HALO, HALO)
            for c in whole + rims:
                lanes = slice(c * TILE, (c + 1) * TILE)
                if h == 0:
                    work[f, c, outer] += (
                        top * before[2 * f : 2 * f + 1, lanes] + top_next * before[2 * f + 1 : 2 * f + 2, lanes]
                    )
                else:
                    work[f, c, outer] -= (
                        bottom * after[2 * f : 2 * f + 1, lanes] + bottom_next * after[2 * f + 1 : 2 * f + 2, lanes]
                    )
            for c in whole + rims + middles:
                rows = outer
                if c in whole:
                    rows = pl.ds(h * half, half)
                elif c in middles:
                    rows = pl.ds(HALO if h == 0 else half, half - HALO)
                copy = pltpu.make_async_copy(
                    work.at[f, c, rows], out_hbm.at[f, rows, pl.ds(c * TILE, TILE)], sems.at[f, c, h]
                )
                copy.start()
                copies.append(copy)
    for copy in copies:
        copy.wait()


def half_kernel(pad, inner, far_z, out_hbm, work, turned_in, turned_out, sems):
    @pl.when(place_z() == 1)
    def _():
        halo_columns(jnp.zeros((EDGE, TILE), jnp.float32), far_z[0:EDGE], turned_in, turned_out)
        finish((), (), (1,), False, pad, inner, None, None, out_hbm, work, turned_out, sems)


def edge_kernel(pad, inner, near_x, far_x, far_z, near_z, half, out_hbm, work, turned_in, turned_out, sems):
    even_x, even_z = is_even("gx"), is_even("gz")
    before = jnp.where(even_x, far_x[...], near_x[...])
    after = jnp.where(even_x, near_x[...], far_x[...])
    near, far = near_z[...], far_z[0:EDGE]
    halo_columns(jnp.where(even_z, far, near), jnp.where(even_z, near, far), turned_in, turned_out)
    rest = (pad, inner, before, after, out_hbm, work, turned_out, sems)
    pl.when(place_z() == 0)(lambda: finish((0, 1), (), (), False, *rest))
    pl.when(place_z() == 1)(lambda: finish((0,), (1,), (), False, *rest))
    pl.when(place_z() > 1)(lambda: finish((0, 1), (), (), True, *rest))


def vmem_spec():
    return pl.BlockSpec(memory_space=pltpu.VMEM)


def any_spec():
    return pl.BlockSpec(memory_space=pl.ANY)


def in_vmem(value):
    return pltpu.with_memory_space_constraint(value, pltpu.VMEM)


def call(kernel, outs, scratch, ins, name, aliases=None, out_specs=None):
    return pl.pallas_call(
        kernel,
        out_shape=outs,
        in_specs=[any_spec() if value.ndim == 3 else vmem_spec() for value in ins],
        out_specs=out_specs or (vmem_spec(),) * len(outs),
        scratch_shapes=scratch,
        input_output_aliases=aliases or {},
        compiler_params=pltpu.CompilerParams(vmem_limit_bytes=16 * MIB),
        name=name,
    )(*ins)


def on_device(velocity):
    f32 = jnp.float32
    block = pltpu.VMEM((FIELDS, 2, LONG, TILE), f32)
    x_edge, z_edge = pltpu.VMEM((2 * FIELDS, LANES), f32), pltpu.VMEM((EDGE, TILE), f32)
    far_edge = pltpu.VMEM((FAR_EDGE, TILE), f32)
    turned = pltpu.VMEM((400, TILE), f32)
    swept = [pltpu.VMEM((2 * FIELDS, STEPS * SUB, TILE), f32)]
    pad, z_part, near_x, far_x, near_z, far_z = call(
        pack_kernel,
        (
            pltpu.VMEM((FIELDS, 2, PAD, TILE), f32),
            pltpu.VMEM((EARLY, 2, LONG, TILE), f32),
            x_edge,
            x_edge,
            z_edge,
            far_edge,
        ),
        [turned, turned, pltpu.SemaphoreType.DMA((FIELDS, 2))],
        [pltpu.with_memory_space_constraint(velocity, pltpu.HBM)],
        "pack",
    )

    def swap(value, axis, first):
        size = lax.axis_size(axis)
        pairs = [(i % size, (i + 1) % size) for i in range(first, size, 2)]
        return lax.ppermute(value, axis, pairs + [(j, i) for i, j in pairs])

    pad, z_part = in_vmem(pad), in_vmem(z_part)
    partial, far_z = call(first_kernel, (block, far_edge), swept, [pad, z_part, in_vmem(far_z)], "first", {2: 1})
    far_z = swap(far_z, "gz", 1)
    partial, near_z, near_x, far_x = call(
        second_kernel,
        (block, z_edge, x_edge, x_edge),
        swept,
        [pad, z_part, in_vmem(partial), in_vmem(near_z), in_vmem(near_x), in_vmem(far_x)],
        "second",
        {2: 0, 3: 1, 4: 2, 5: 3},
    )
    near_z = swap(near_z, "gz", 0)
    near_x, far_x = swap(near_x, "gx", 0), swap(far_x, "gx", 1)
    (partial,) = call(inner_kernel, (block,), swept, [pad, z_part, in_vmem(partial)], "inner", {2: 0})
    partial = in_vmem(partial)
    work = [
        pltpu.VMEM((FIELDS, 2, ROWS, TILE), f32),
        pltpu.VMEM((2 * EDGE, TILE), f32),
        turned,
        pltpu.SemaphoreType.DMA((FIELDS, 2, 2)),
    ]
    whole = pltpu.HBM((FIELDS, ROWS, LANES), f32)
    half = call(half_kernel, whole, work, [pad, partial, far_z], "half", None, any_spec())
    return call(
        edge_kernel,
        whole,
        work,
        [pad, partial, near_x, far_x, far_z, near_z, half],
        "edges",
        {6: 0},
        any_spec(),
    )


def solution(mesh):
    return jax.shard_map(
        on_device,
        mesh=mesh,
        in_specs=(P(None, "gx", "gz"),),
        out_specs=P(None, "gx", "gz"),
        check_vma=False,
    )
```

```python
import math

import jax
import jax.numpy as jnp
import numpy as np
from jax import lax
from jax.experimental import pallas as pl
from jax.experimental.pallas import tpu as pltpu
from jax.sharding import PartitionSpec as P

FIELDS, ROWS, LANES = 4, 1536, 256
HALO = 24
PAD = 1576
SUB = 8
CHUNK = ROWS // SUB + 1
WARM = HALO - 2
STEPS = 216
UNROLL = 8
EARLY = 1
MIDDLE = 2
LONG = SUB * CHUNK
TILE = 128
BLOCKS = ROWS // TILE
TILE_ROWS = FIELDS * BLOCKS
RATIO = (math.sqrt(5.0) - 3.0) / 2.0
KAPPA = -1.0 / (3.0 * RATIO)
NEAR = 7.0 / 9.0 / KAPPA
FAR = 1.0 / 36.0 / KAPPA
MIB = 1 << 20


GAP = TILE_ROWS + 1
EDGE = 152
FAR_EDGE = 160
SCALE = 1.0 / (KAPPA * (1.0 - RATIO * RATIO))
TAIL = SCALE * (7.0 / 9.0 * (RATIO - 1.0 / RATIO) + 1.0 / 36.0 * (RATIO**2 - RATIO**-2))
NEXT = -1.0 / 12.0


def powers(exponent):
    value = jnp.where(exponent % 2 == 1, RATIO, 1.0)
    for bit in (2, 4, 8, 16):
        value = value * jnp.where((exponent // bit) % 2 == 1, RATIO**bit, 1.0)
    return value


def difference_matrix():
    gap = lax.broadcasted_iota(jnp.int32, (LANES, LANES), 0) - lax.broadcasted_iota(
        jnp.int32, (LANES, LANES), 1
    )
    size = jnp.abs(gap)
    weight = jnp.where(size == 1, 45.0, jnp.where(size == 2, -9.0, jnp.where(size == 3, 1.0, 0.0)))
    return jnp.where(gap < 0, -weight, weight).astype(jnp.bfloat16)


def spanwise(here, matrix):
    high = here.astype(jnp.bfloat16)
    rest = here - high.astype(jnp.float32)
    middle = rest.astype(jnp.bfloat16)
    low = (rest - middle.astype(jnp.float32)).astype(jnp.bfloat16)
    total = jnp.dot(high, matrix, preferred_element_type=jnp.float32)
    total += jnp.dot(middle, matrix, preferred_element_type=jnp.float32)
    total += jnp.dot(low, matrix, preferred_element_type=jnp.float32)
    return total * (1.0 / 60.0)


def field_rows(pad, f, row, count):
    rows = pl.ds(HALO + row, count)
    return jnp.concatenate([pad[f, 0, rows], pad[f, 1, rows]], axis=1)


def is_even(axis):
    return lax.rem(lax.axis_index(axis), 2) == 0


def fetch(v_hbm, pad, sides, sems):
    copies = {}
    for f in range(FIELDS):
        for c in sides:
            lanes = pl.ds(c * TILE, TILE)
            copies[f, c] = pltpu.make_async_copy(v_hbm.at[f, :, lanes], pad.at[f, c, pl.ds(HALO, ROWS)], sems.at[f, c])
            copies[f, c].start()

    def wait(f):
        for c in sides:
            copies[f, c].wait()

    return wait


def pack_x(f, pad, near_x, far_x):
    even_x = is_even("gx")
    place = lax.broadcasted_iota(jnp.int32, (HALO, TILE), 0)
    head_weight, tail_weight = powers(place + 1), powers(HALO - place)
    for c in range(2):
        lanes = pl.ds(c * TILE, TILE)
        head, tail = pad[f, c, pl.ds(HALO, HALO)], pad[f, c, pl.ds(ROWS, HALO)]
        head_sum = jnp.sum(head * head_weight, axis=0, keepdims=True)
        tail_sum = jnp.sum(tail * tail_weight, axis=0, keepdims=True)
        near_x[pl.ds(2 * f, 1), lanes] = jnp.where(even_x, tail_sum, head_sum)
        far_x[pl.ds(2 * f, 1), lanes] = jnp.where(even_x, head_sum, tail_sum)
        near_x[pl.ds(2 * f + 1, 1), lanes] = jnp.where(even_x, tail[HALO - 1 :], head[:1])
        far_x[pl.ds(2 * f + 1, 1), lanes] = jnp.where(even_x, head[:1], tail[HALO - 1 :])


def turn(f, pad, sides, turned_first, turned_last):
    lane = lax.broadcasted_iota(jnp.int32, (TILE, TILE), 1)
    for b in range(BLOCKS):
        rows = pl.ds(HALO + b * TILE, TILE)
        tile = pad[f, sides[0], rows]
        if len(sides) == 2:
            tile = jnp.where(lane < 64, tile, pad[f, 1, rows])
        turned = tile.T
        block = f * BLOCKS + b
        if 0 in sides:
            turned_first[pl.ds(block, SUB, stride=GAP)] = turned[:SUB]
        if 1 in sides:
            turned_last[pl.ds(block + 3, SUB, stride=GAP)] = turned[TILE - SUB :]


def early_spanwise(f, pad, z_part):
    if f >= EARLY:
        return
    matrix = difference_matrix()
    for b in range(0, ROWS, 256):
        total = spanwise(field_rows(pad, f, b, 256), matrix)
        z_part[f, 0, pl.ds(b, 256)] = total[:, :TILE]
        z_part[f, 1, pl.ds(b, 256)] = total[:, TILE:]


def last_columns(turned_last):
    return turned_last[5 * GAP + 3 : 5 * GAP + 3 + EDGE]


def is_awaited():
    return place_z() == lax.axis_size("gz") - 1


def pack_kernel(v_hbm, pad, z_part, near_x, far_x, near_z, far_z, turned_first, turned_last, sems):
    zeros = jnp.zeros((HALO, TILE), jnp.float32)
    for f in range(FIELDS):
        for c in range(2):
            pad[f, c, pl.ds(0, HALO)] = zeros
            pad[f, c, pl.ds(HALO + ROWS, PAD - HALO - ROWS)] = jnp.zeros((PAD - HALO - ROWS, TILE), jnp.float32)
    far_z[EDGE:] = jnp.zeros((FAR_EDGE - EDGE, TILE), jnp.float32)

    @pl.when(is_awaited())
    def _():
        wait = fetch(v_hbm, pad, (1,), sems)
        for f in range(FIELDS):
            wait(f)
            turn(f, pad, (1,), turned_first, turned_last)
        far_z[0:EDGE] = last_columns(turned_last)

    @pl.when(jnp.logical_not(is_awaited()))
    def _():
        wait = fetch(v_hbm, pad, (0, 1), sems)
        for f in range(FIELDS):
            wait(f)
            pack_x(f, pad, near_x, far_x)
            turn(f, pad, (0, 1), turned_first, turned_last)
            early_spanwise(f, pad, z_part)
        even_z = is_even("gz")
        first, last = turned_first[0:EDGE], last_columns(turned_last)
        near_z[...] = jnp.where(even_z, last, first)
        far_z[0:EDGE] = jnp.where(even_z, first, last)


def inner_body(pad, z_part, out, swept):
    chains = [(f, c) for f in range(FIELDS) for c in (0, 1)]
    count = len(chains)

    def row(chain, k):
        f, c = chain
        return pad[f, c, pl.ds(k, SUB, stride=CHUNK)]

    def forward(step, carry):
        carry = list(carry)
        for u in range(UNROLL):
            k = step * UNROLL + u
            for n, chain in enumerate(chains):
                back2, back1, here, ahead1, y = carry[n]
                ahead2 = row(chain, k + 4)
                y = RATIO * y + (NEAR * (ahead1 - back1) + FAR * (ahead2 - back2))
                swept[n, pl.ds(pl.multiple_of(k * SUB, SUB), SUB)] = y
                carry[n] = (back1, here, ahead1, ahead2, y)
        return tuple(carry)

    zero = jnp.zeros((SUB, TILE), jnp.float32)
    start = tuple(tuple(row(chain, j) for j in range(4)) + (zero,) for chain in chains)
    lax.fori_loop(0, STEPS // UNROLL, forward, start)

    def value(n, k):
        return swept[n, pl.ds(pl.multiple_of(k * SUB, SUB), SUB)]

    carry = [zero] * count
    for k in range(WARM - 1, -1, -1):
        carry = [RATIO * carry[n] + value(n, k + WARM) for n in range(count)]
    sub = lax.broadcasted_iota(jnp.int32, (SUB, TILE), 0)
    beyond = RATIO / (1.0 - RATIO * RATIO)
    carry = [
        jnp.where(sub == SUB - 1, beyond * value(n, WARM + CHUNK - 1), pltpu.roll(carry[n], SUB - 1, 0))
        for n in range(count)
    ]

    def back(carry, k):
        carry = [RATIO * carry[n] + value(n, k + WARM) for n in range(count)]
        for n, (f, c) in enumerate(chains):
            at = pl.ds(k, SUB, stride=CHUNK)
            out[f, c, at] = carry[n] + z_part[f, c, at] if f < EARLY else carry[n]
        return carry

    def backward(step, carry):
        for u in range(UNROLL):
            carry = back(carry, CHUNK - 2 - (step * UNROLL + u))
        return tuple(carry)

    lax.fori_loop(0, CHUNK // UNROLL, backward, tuple(back(carry, CHUNK - 1)))
    add_spanwise(pad, out, range(EARLY, MIDDLE))


def add_spanwise(pad, out, fields):
    matrix = difference_matrix()
    for f in fields:
        for b in range(0, ROWS, 256):
            total = spanwise(field_rows(pad, f, b, 256), matrix)
            out[f, 0, pl.ds(b, 256)] += total[:, :TILE]
            out[f, 1, pl.ds(b, 256)] += total[:, TILE:]


def place_z():
    return lax.axis_index("gz")


def first_kernel(pad, z_part, far_z_in, out, far_z, swept):
    pl.when(place_z() == 0)(lambda: inner_body(pad, z_part, out, swept))


def second_kernel(
    pad_in, z_part_in, done, near_z_in, near_x_in, far_x_in, v_hbm,
    out, near_z, near_x, far_x, pad, z_part, swept, turned_first, turned_last, sems,
):
    @pl.when(place_z() == 1)
    def _():
        inner_body(pad, z_part, out, swept)
        add_spanwise(pad, out, range(MIDDLE, FIELDS))

    @pl.when(is_awaited())
    def _():
        wait = fetch(v_hbm, pad, (0,), sems)
        for f in range(FIELDS):
            wait(f)
            pack_x(f, pad, near_x, far_x)
            turn(f, pad, (0,), turned_first, turned_last)
            early_spanwise(f, pad, z_part)
        near_z[...] = turned_first[0:EDGE]


def inner_kernel(pad, z_part, done, out, swept):
    pl.when(place_z() > 1)(lambda: inner_body(pad, z_part, out, swept))
    pl.when(place_z() == 0)(lambda: add_spanwise(pad, out, range(MIDDLE, FIELDS)))


def halo_columns(left, right, turned_in, turned_out):
    turned_in[0:EDGE] = left
    turned_in[EDGE:] = right
    l3, l2, l1 = (turned_in[n * GAP : n * GAP + TILE_ROWS] for n in range(3))
    r1, r2, r3 = (turned_in[EDGE + n * GAP : EDGE + n * GAP + TILE_ROWS] for n in range(3))
    none = jnp.zeros((TILE_ROWS, TILE), jnp.float32)
    for n, value in enumerate(
        (
            -0.75 * l1 + 0.15 * l2 - l3 * (1.0 / 60.0),
            0.15 * l1 - l2 * (1.0 / 60.0),
            l1 * (-1.0 / 60.0),
            none,
            none,
            r1 * (1.0 / 60.0),
            -0.15 * r1 + r2 * (1.0 / 60.0),
            0.75 * r1 - 0.15 * r2 + r3 * (1.0 / 60.0),
        )
    ):
        turned_out[n * GAP : n * GAP + TILE_ROWS] = value


def finish(whole, rims, middles, late, pad, inner, before, after, out_hbm, work, turned_out, sems):
    copies = []
    matrix = difference_matrix()
    place = lax.broadcasted_iota(jnp.int32, (HALO, TILE), 0)
    top, bottom = TAIL * powers(place), TAIL * powers(HALO - 1 - place)
    top_next, bottom_next = jnp.where(place == 0, NEXT, 0.0), jnp.where(place == HALO - 1, NEXT, 0.0)
    zeros = jnp.zeros((TILE - 2 * SUB, TILE), jnp.float32)
    lane = lax.broadcasted_iota(jnp.int32, (TILE, TILE), 1)
    own = (lane < 4, lane >= TILE - 4)
    half = ROWS // 2
    for f in range(FIELDS):
        for h in range(2):
            for b in range(h * BLOCKS // 2, (h + 1) * BLOCKS // 2):
                rows = pl.ds(b * TILE, TILE)
                columns = turned_out[pl.ds(f * BLOCKS + b, SUB, stride=GAP)]
                turned = jnp.concatenate([columns, zeros, columns]).T
                if late and f >= MIDDLE:
                    total = spanwise(field_rows(pad, f, b * TILE, TILE), matrix)
                for c in whole + middles + (rims if b in (0, BLOCKS - 1) else ()):
                    value = inner[f, c, rows]
                    if late and f >= MIDDLE:
                        value = value + total[:, c * TILE : (c + 1) * TILE]
                    work[f, c, rows] = value + jnp.where(own[c], turned, 0.0)
            outer = pl.ds(0, HALO) if h == 0 else pl.ds(ROWS - HALO, HALO)
            for c in whole + rims:
                lanes = slice(c * TILE, (c + 1) * TILE)
                if h == 0:
                    work[f, c, outer] += (
                        top * before[2 * f : 2 * f + 1, lanes] + top_next * before[2 * f + 1 : 2 * f + 2, lanes]
                    )
                else:
                    work[f, c, outer] -= (
                        bottom * after[2 * f : 2 * f + 1, lanes] + bottom_next * after[2 * f + 1 : 2 * f + 2, lanes]
                    )
            for c in whole + rims + middles:
                rows = outer
                if c in whole:
                    rows = pl.ds(h * half, half)
                elif c in middles:
                    rows = pl.ds(HALO if h == 0 else half, half - HALO)
                copy = pltpu.make_async_copy(
                    work.at[f, c, rows], out_hbm.at[f, rows, pl.ds(c * TILE, TILE)], sems.at[f, c, h]
                )
                copy.start()
                copies.append(copy)
    for copy in copies:
        copy.wait()


def half_kernel(pad, inner, far_z, out_hbm, work, turned_in, turned_out, sems):
    @pl.when(place_z() == 1)
    def _():
        halo_columns(jnp.zeros((EDGE, TILE), jnp.float32), far_z[0:EDGE], turned_in, turned_out)
        finish((), (), (1,), False, pad, inner, None, None, out_hbm, work, turned_out, sems)


def edge_kernel(pad, inner, near_x, far_x, far_z, near_z, half, out_hbm, work, turned_in, turned_out, sems):
    even_x, even_z = is_even("gx"), is_even("gz")
    before = jnp.where(even_x, far_x[...], near_x[...])
    after = jnp.where(even_x, near_x[...], far_x[...])
    near, far = near_z[...], far_z[0:EDGE]
    halo_columns(jnp.where(even_z, far, near), jnp.where(even_z, near, far), turned_in, turned_out)
    rest = (pad, inner, before, after, out_hbm, work, turned_out, sems)
    pl.when(place_z() == 0)(lambda: finish((0, 1), (), (), False, *rest))
    pl.when(place_z() == 1)(lambda: finish((0,), (1,), (), False, *rest))
    pl.when(place_z() > 1)(lambda: finish((0, 1), (), (), True, *rest))


def vmem_spec():
    return pl.BlockSpec(memory_space=pltpu.VMEM)


def any_spec():
    return pl.BlockSpec(memory_space=pl.ANY)


def in_vmem(value):
    return pltpu.with_memory_space_constraint(value, pltpu.VMEM)


def call(kernel, outs, scratch, ins, name, aliases=None, out_specs=None):
    return pl.pallas_call(
        kernel,
        out_shape=outs,
        in_specs=[any_spec() if value.ndim == 3 else vmem_spec() for value in ins],
        out_specs=out_specs or (vmem_spec(),) * len(outs),
        scratch_shapes=scratch,
        input_output_aliases=aliases or {},
        compiler_params=pltpu.CompilerParams(vmem_limit_bytes=16 * MIB),
        name=name,
    )(*ins)


def on_device(velocity):
    f32 = jnp.float32
    block = pltpu.VMEM((FIELDS, 2, LONG, TILE), f32)
    x_edge, z_edge = pltpu.VMEM((2 * FIELDS, LANES), f32), pltpu.VMEM((EDGE, TILE), f32)
    far_edge = pltpu.VMEM((FAR_EDGE, TILE), f32)
    turned = pltpu.VMEM((400, TILE), f32)
    swept = [pltpu.VMEM((2 * FIELDS, STEPS * SUB, TILE), f32)]
    packing = [turned, turned, pltpu.SemaphoreType.DMA((FIELDS, 2))]
    pad_type = pltpu.VMEM((FIELDS, 2, PAD, TILE), f32)
    z_part_type = pltpu.VMEM((EARLY, 2, LONG, TILE), f32)
    source = pltpu.with_memory_space_constraint(velocity, pltpu.HBM)
    pad, z_part, near_x, far_x, near_z, far_z = call(
        pack_kernel, (pad_type, z_part_type, x_edge, x_edge, z_edge, far_edge), packing, [source], "pack"
    )

    def swap(value, axis, first):
        size = lax.axis_size(axis)
        pairs = [(i % size, (i + 1) % size) for i in range(first, size, 2)]
        return lax.ppermute(value, axis, pairs + [(j, i) for i, j in pairs])

    pad, z_part = in_vmem(pad), in_vmem(z_part)
    partial, far_z = call(first_kernel, (block, far_edge), swept, [pad, z_part, in_vmem(far_z)], "first", {2: 1})
    far_z = swap(far_z, "gz", 1)
    partial, near_z, near_x, far_x, pad, z_part = call(
        second_kernel,
        (block, z_edge, x_edge, x_edge, pad_type, z_part_type),
        swept + packing,
        [pad, z_part, in_vmem(partial), in_vmem(near_z), in_vmem(near_x), in_vmem(far_x), source],
        "second",
        {2: 0, 3: 1, 4: 2, 5: 3, 0: 4, 1: 5},
    )
    pad, z_part = in_vmem(pad), in_vmem(z_part)
    near_z = swap(near_z, "gz", 0)
    near_x, far_x = swap(near_x, "gx", 0), swap(far_x, "gx", 1)
    (partial,) = call(inner_kernel, (block,), swept, [pad, z_part, in_vmem(partial)], "inner", {2: 0})
    partial = in_vmem(partial)
    work = [
        pltpu.VMEM((FIELDS, 2, ROWS, TILE), f32),
        pltpu.VMEM((2 * EDGE, TILE), f32),
        turned,
        pltpu.SemaphoreType.DMA((FIELDS, 2, 2)),
    ]
    whole = pltpu.HBM((FIELDS, ROWS, LANES), f32)
    half = call(half_kernel, whole, work, [pad, partial, far_z], "half", None, any_spec())
    return call(
        edge_kernel,
        whole,
        work,
        [pad, partial, near_x, far_x, far_z, near_z, half],
        "edges",
        {6: 0},
        any_spec(),
    )


def solution(mesh):
    return jax.shard_map(
        on_device,
        mesh=mesh,
        in_specs=(P(None, "gx", "gz"),),
        out_specs=P(None, "gx", "gz"),
        check_vma=False,
    )
```

```python
import math

import jax
import jax.numpy as jnp
import numpy as np
from jax import lax
from jax.experimental import pallas as pl
from jax.experimental.pallas import tpu as pltpu
from jax.sharding import PartitionSpec as P

FIELDS, ROWS, LANES = 4, 1536, 256
HALO = 24
PAD = 1576
SUB = 8
CHUNK = ROWS // SUB + 1
WARM = HALO - 2
STEPS = 216
UNROLL = 8
EARLY = 1
MIDDLE = 2
LONG = SUB * CHUNK
TILE = 128
BLOCKS = ROWS // TILE
TILE_ROWS = FIELDS * BLOCKS
RATIO = (math.sqrt(5.0) - 3.0) / 2.0
KAPPA = -1.0 / (3.0 * RATIO)
NEAR = 7.0 / 9.0 / KAPPA
FAR = 1.0 / 36.0 / KAPPA
MIB = 1 << 20


GAP = TILE_ROWS + 1
EDGE = 152
FAR_EDGE = 160
SCALE = 1.0 / (KAPPA * (1.0 - RATIO * RATIO))
TAIL = SCALE * (7.0 / 9.0 * (RATIO - 1.0 / RATIO) + 1.0 / 36.0 * (RATIO**2 - RATIO**-2))
NEXT = -1.0 / 12.0


def powers(exponent):
    value = jnp.where(exponent % 2 == 1, RATIO, 1.0)
    for bit in (2, 4, 8, 16):
        value = value * jnp.where((exponent // bit) % 2 == 1, RATIO**bit, 1.0)
    return value


def difference_matrix():
    gap = lax.broadcasted_iota(jnp.int32, (LANES, LANES), 0) - lax.broadcasted_iota(
        jnp.int32, (LANES, LANES), 1
    )
    size = jnp.abs(gap)
    weight = jnp.where(size == 1, 45.0, jnp.where(size == 2, -9.0, jnp.where(size == 3, 1.0, 0.0)))
    return jnp.where(gap < 0, -weight, weight).astype(jnp.bfloat16)


def spanwise(here, matrix):
    high = here.astype(jnp.bfloat16)
    rest = here - high.astype(jnp.float32)
    middle = rest.astype(jnp.bfloat16)
    low = (rest - middle.astype(jnp.float32)).astype(jnp.bfloat16)
    total = jnp.dot(high, matrix, preferred_element_type=jnp.float32)
    total += jnp.dot(middle, matrix, preferred_element_type=jnp.float32)
    total += jnp.dot(low, matrix, preferred_element_type=jnp.float32)
    return total * (1.0 / 60.0)


def field_rows(pad, f, row, count):
    rows = pl.ds(HALO + row, count)
    return jnp.concatenate([pad[f, 0, rows], pad[f, 1, rows]], axis=1)


def is_even(axis):
    return lax.rem(lax.axis_index(axis), 2) == 0


def pack_kernel(v_hbm, pad, z_part, near_x, far_x, near_z, far_z, turned_first, turned_last, sems):
    copies = []
    for f in range(FIELDS):
        for c in range(2):
            lanes = pl.ds(c * TILE, TILE)
            copy = pltpu.make_async_copy(v_hbm.at[f, :, lanes], pad.at[f, c, pl.ds(HALO, ROWS)], sems.at[f, c])
            copy.start()
            copies.append(copy)
    even_x, even_z = is_even("gx"), is_even("gz")
    matrix = difference_matrix()
    zeros = jnp.zeros((HALO, TILE), jnp.float32)
    for f in range(FIELDS):
        for c in range(2):
            pad[f, c, pl.ds(0, HALO)] = zeros
            pad[f, c, pl.ds(HALO + ROWS, PAD - HALO - ROWS)] = jnp.zeros((PAD - HALO - ROWS, TILE), jnp.float32)
    lane = lax.broadcasted_iota(jnp.int32, (TILE, TILE), 1)
    place = lax.broadcasted_iota(jnp.int32, (HALO, TILE), 0)
    head_weight, tail_weight = powers(place + 1), powers(HALO - place)
    for f in range(FIELDS):
        for c in range(2):
            copies[2 * f + c].wait()
        for c in range(2):
            lanes = pl.ds(c * TILE, TILE)
            head, tail = pad[f, c, pl.ds(HALO, HALO)], pad[f, c, pl.ds(ROWS, HALO)]
            head_sum = jnp.sum(head * head_weight, axis=0, keepdims=True)
            tail_sum = jnp.sum(tail * tail_weight, axis=0, keepdims=True)
            near_x[pl.ds(2 * f, 1), lanes] = jnp.where(even_x, tail_sum, head_sum)
            far_x[pl.ds(2 * f, 1), lanes] = jnp.where(even_x, head_sum, tail_sum)
            near_x[pl.ds(2 * f + 1, 1), lanes] = jnp.where(even_x, tail[HALO - 1 :], head[:1])
            far_x[pl.ds(2 * f + 1, 1), lanes] = jnp.where(even_x, head[:1], tail[HALO - 1 :])
        for b in range(BLOCKS):
            rows = pl.ds(HALO + b * TILE, TILE)
            turned = jnp.where(lane < 64, pad[f, 0, rows], pad[f, 1, rows]).T
            block = f * BLOCKS + b
            turned_first[pl.ds(block, SUB, stride=GAP)] = turned[:SUB]
            turned_last[pl.ds(block + 3, SUB, stride=GAP)] = turned[TILE - SUB :]
        if f < EARLY:
            for b in range(0, ROWS, 256):
                total = spanwise(field_rows(pad, f, b, 256), matrix)
                z_part[f, 0, pl.ds(b, 256)] = total[:, :TILE]
                z_part[f, 1, pl.ds(b, 256)] = total[:, TILE:]
    first, last = turned_first[0:EDGE], turned_last[5 * GAP + 3 : 5 * GAP + 3 + EDGE]
    near_z[...] = jnp.where(even_z, last, first)
    far_z[0:EDGE] = jnp.where(even_z, first, last)
    far_z[EDGE:] = jnp.zeros((FAR_EDGE - EDGE, TILE), jnp.float32)


def inner_body(pad, z_part, out, swept):
    chains = [(f, c) for f in range(FIELDS) for c in (0, 1)]
    count = len(chains)

    def row(chain, k):
        f, c = chain
        return pad[f, c, pl.ds(k, SUB, stride=CHUNK)]

    def forward(step, carry):
        carry = list(carry)
        for u in range(UNROLL):
            k = step * UNROLL + u
            for n, chain in enumerate(chains):
                back2, back1, here, ahead1, y = carry[n]
                ahead2 = row(chain, k + 4)
                y = RATIO * y + (NEAR * (ahead1 - back1) + FAR * (ahead2 - back2))
                swept[n, pl.ds(pl.multiple_of(k * SUB, SUB), SUB)] = y
                carry[n] = (back1, here, ahead1, ahead2, y)
        return tuple(carry)

    zero = jnp.zeros((SUB, TILE), jnp.float32)
    start = tuple(tuple(row(chain, j) for j in range(4)) + (zero,) for chain in chains)
    lax.fori_loop(0, STEPS // UNROLL, forward, start)

    def value(n, k):
        return swept[n, pl.ds(pl.multiple_of(k * SUB, SUB), SUB)]

    carry = [zero] * count
    for k in range(WARM - 1, -1, -1):
        carry = [RATIO * carry[n] + value(n, k + WARM) for n in range(count)]
    sub = lax.broadcasted_iota(jnp.int32, (SUB, TILE), 0)
    beyond = RATIO / (1.0 - RATIO * RATIO)
    carry = [
        jnp.where(sub == SUB - 1, beyond * value(n, WARM + CHUNK - 1), pltpu.roll(carry[n], SUB - 1, 0))
        for n in range(count)
    ]

    def back(carry, k):
        carry = [RATIO * carry[n] + value(n, k + WARM) for n in range(count)]
        for n, (f, c) in enumerate(chains):
            at = pl.ds(k, SUB, stride=CHUNK)
            out[f, c, at] = carry[n] + z_part[f, c, at] if f < EARLY else carry[n]
        return carry

    def backward(step, carry):
        for u in range(UNROLL):
            carry = back(carry, CHUNK - 2 - (step * UNROLL + u))
        return tuple(carry)

    lax.fori_loop(0, CHUNK // UNROLL, backward, tuple(back(carry, CHUNK - 1)))
    add_spanwise(pad, out, range(EARLY, MIDDLE))


def add_spanwise(pad, out, fields):
    matrix = difference_matrix()
    for f in fields:
        for b in range(0, ROWS, 256):
            total = spanwise(field_rows(pad, f, b, 256), matrix)
            out[f, 0, pl.ds(b, 256)] += total[:, :TILE]
            out[f, 1, pl.ds(b, 256)] += total[:, TILE:]


def place_z():
    return lax.axis_index("gz")


def first_kernel(pad, z_part, far_z_in, out, far_z, swept):
    pl.when(place_z() == 0)(lambda: inner_body(pad, z_part, out, swept))


def second_kernel(pad, z_part, done, near_z_in, near_x_in, far_x_in, out, near_z, near_x, far_x, swept):
    @pl.when(place_z() == 1)
    def _():
        inner_body(pad, z_part, out, swept)
        add_spanwise(pad, out, range(MIDDLE, FIELDS))


def inner_kernel(pad, z_part, done, out, swept):
    pl.when(place_z() > 1)(lambda: inner_body(pad, z_part, out, swept))


def halo_columns(left, right, turned_in, turned_out):
    turned_in[0:EDGE] = left
    turned_in[EDGE:] = right
    l3, l2, l1 = (turned_in[n * GAP : n * GAP + TILE_ROWS] for n in range(3))
    r1, r2, r3 = (turned_in[EDGE + n * GAP : EDGE + n * GAP + TILE_ROWS] for n in range(3))
    none = jnp.zeros((TILE_ROWS, TILE), jnp.float32)
    for n, value in enumerate(
        (
            -0.75 * l1 + 0.15 * l2 - l3 * (1.0 / 60.0),
            0.15 * l1 - l2 * (1.0 / 60.0),
            l1 * (-1.0 / 60.0),
            none,
            none,
            r1 * (1.0 / 60.0),
            -0.15 * r1 + r2 * (1.0 / 60.0),
            0.75 * r1 - 0.15 * r2 + r3 * (1.0 / 60.0),
        )
    ):
        turned_out[n * GAP : n * GAP + TILE_ROWS] = value


def finish(whole, rims, middles, late, pad, inner, before, after, out_hbm, work, turned_out, sems):
    copies = []
    matrix = difference_matrix()
    place = lax.broadcasted_iota(jnp.int32, (HALO, TILE), 0)
    top, bottom = TAIL * powers(place), TAIL * powers(HALO - 1 - place)
    top_next, bottom_next = jnp.where(place == 0, NEXT, 0.0), jnp.where(place == HALO - 1, NEXT, 0.0)
    zeros = jnp.zeros((TILE - 2 * SUB, TILE), jnp.float32)
    lane = lax.broadcasted_iota(jnp.int32, (TILE, TILE), 1)
    own = (lane < 4, lane >= TILE - 4)
    half = ROWS // 2
    for f in range(FIELDS):
        for h in range(2):
            for b in range(h * BLOCKS // 2, (h + 1) * BLOCKS // 2):
                rows = pl.ds(b * TILE, TILE)
                columns = turned_out[pl.ds(f * BLOCKS + b, SUB, stride=GAP)]
                turned = jnp.concatenate([columns, zeros, columns]).T
                if late and f >= MIDDLE:
                    total = spanwise(field_rows(pad, f, b * TILE, TILE), matrix)
                for c in whole + middles + (rims if b in (0, BLOCKS - 1) else ()):
                    value = inner[f, c, rows]
                    if late and f >= MIDDLE:
                        value = value + total[:, c * TILE : (c + 1) * TILE]
                    work[f, c, rows] = value + jnp.where(own[c], turned, 0.0)
            outer = pl.ds(0, HALO) if h == 0 else pl.ds(ROWS - HALO, HALO)
            for c in whole + rims:
                lanes = slice(c * TILE, (c + 1) * TILE)
                if h == 0:
                    work[f, c, outer] += (
                        top * before[2 * f : 2 * f + 1, lanes] + top_next * before[2 * f + 1 : 2 * f + 2, lanes]
                    )
                else:
                    work[f, c, outer] -= (
                        bottom * after[2 * f : 2 * f + 1, lanes] + bottom_next * after[2 * f + 1 : 2 * f + 2, lanes]
                    )
            for c in whole + rims + middles:
                rows = outer
                if c in whole:
                    rows = pl.ds(h * half, half)
                elif c in middles:
                    rows = pl.ds(HALO if h == 0 else half, half - HALO)
                copy = pltpu.make_async_copy(
                    work.at[f, c, rows], out_hbm.at[f, rows, pl.ds(c * TILE, TILE)], sems.at[f, c, h]
                )
                copy.start()
                copies.append(copy)
    for copy in copies:
        copy.wait()


def half_kernel(pad, inner, far_z, out_hbm, work, turned_in, turned_out, sems):
    @pl.when(place_z() == 1)
    def _():
        halo_columns(jnp.zeros((EDGE, TILE), jnp.float32), far_z[0:EDGE], turned_in, turned_out)
        finish((), (), (1,), False, pad, inner, None, None, out_hbm, work, turned_out, sems)


def edge_kernel(pad, inner, far_z, near_z, far_x, near_x, half, out_hbm, work, turned_in, turned_out, sems):
    even_x, even_z = is_even("gx"), is_even("gz")
    before = jnp.where(even_x, far_x[...], near_x[...])
    after = jnp.where(even_x, near_x[...], far_x[...])
    near, far = near_z[...], far_z[0:EDGE]
    halo_columns(jnp.where(even_z, far, near), jnp.where(even_z, near, far), turned_in, turned_out)
    rest = (pad, inner, before, after, out_hbm, work, turned_out, sems)
    pl.when(place_z() == 1)(lambda: finish((0,), (1,), (), False, *rest))
    pl.when(place_z() != 1)(lambda: finish((0, 1), (), (), True, *rest))


def vmem_spec():
    return pl.BlockSpec(memory_space=pltpu.VMEM)


def any_spec():
    return pl.BlockSpec(memory_space=pl.ANY)


def in_vmem(value):
    return pltpu.with_memory_space_constraint(value, pltpu.VMEM)


def call(kernel, outs, scratch, ins, name, aliases=None, out_specs=None):
    return pl.pallas_call(
        kernel,
        out_shape=outs,
        in_specs=[any_spec() if value.ndim == 3 else vmem_spec() for value in ins],
        out_specs=out_specs or (vmem_spec(),) * len(outs),
        scratch_shapes=scratch,
        input_output_aliases=aliases or {},
        compiler_params=pltpu.CompilerParams(vmem_limit_bytes=16 * MIB),
        name=name,
    )(*ins)


def on_device(velocity):
    f32 = jnp.float32
    block = pltpu.VMEM((FIELDS, 2, LONG, TILE), f32)
    x_edge, z_edge = pltpu.VMEM((2 * FIELDS, LANES), f32), pltpu.VMEM((EDGE, TILE), f32)
    far_edge = pltpu.VMEM((FAR_EDGE, TILE), f32)
    turned = pltpu.VMEM((400, TILE), f32)
    swept = [pltpu.VMEM((2 * FIELDS, STEPS * SUB, TILE), f32)]
    pad, z_part, near_x, far_x, near_z, far_z = call(
        pack_kernel,
        (
            pltpu.VMEM((FIELDS, 2, PAD, TILE), f32),
            pltpu.VMEM((EARLY, 2, LONG, TILE), f32),
            x_edge,
            x_edge,
            z_edge,
            far_edge,
        ),
        [turned, turned, pltpu.SemaphoreType.DMA((FIELDS, 2))],
        [pltpu.with_memory_space_constraint(velocity, pltpu.HBM)],
        "pack",
    )

    def swap(value, axis, first):
        size = lax.axis_size(axis)
        pairs = [(i % size, (i + 1) % size) for i in range(first, size, 2)]
        return lax.ppermute(value, axis, pairs + [(j, i) for i, j in pairs])

    pad, z_part = in_vmem(pad), in_vmem(z_part)
    partial, far_z = call(first_kernel, (block, far_edge), swept, [pad, z_part, in_vmem(far_z)], "first", {2: 1})
    far_z = swap(far_z, "gz", 1)
    partial, near_z, near_x, far_x = call(
        second_kernel,
        (block, z_edge, x_edge, x_edge),
        swept,
        [pad, z_part, in_vmem(partial), in_vmem(near_z), in_vmem(near_x), in_vmem(far_x)],
        "second",
        {2: 0, 3: 1, 4: 2, 5: 3},
    )
    near_z = swap(near_z, "gz", 0)
    near_x, far_x = swap(near_x, "gx", 0), swap(far_x, "gx", 1)
    (partial,) = call(inner_kernel, (block,), swept, [pad, z_part, in_vmem(partial)], "inner", {2: 0})
    partial = in_vmem(partial)
    work = [
        pltpu.VMEM((FIELDS, 2, ROWS, TILE), f32),
        pltpu.VMEM((2 * EDGE, TILE), f32),
        turned,
        pltpu.SemaphoreType.DMA((FIELDS, 2, 2)),
    ]
    whole = pltpu.HBM((FIELDS, ROWS, LANES), f32)
    half = call(half_kernel, whole, work, [pad, partial, far_z], "half", None, any_spec())
    return call(
        edge_kernel,
        whole,
        work,
        [pad, partial, far_z, near_z, far_x, near_x, half],
        "edges",
        {6: 0},
        any_spec(),
    )


def solution(mesh):
    return jax.shard_map(
        on_device,
        mesh=mesh,
        in_specs=(P(None, "gx", "gz"),),
        out_specs=P(None, "gx", "gz"),
        check_vma=False,
    )
```
